128 devices in a mesh: wide: 8 (over x, y_hi), narrow: 16 (over y_lo, z, core).
Axes of the slice: x: 4, y: 4 (y_hi: 2, y_lo: 2; y = y_hi * 2 + y_lo), z: 4, core: 2. Of those that a mesh axis runs over, the one named last changes fastest.
Arguments:
- tokens: bfloat16 [8192, 4096], P('narrow'), may hold values from -6 to 6
- norm_gain: float32 [4096], replicated, may hold values from 0.1 to 1.9
- coded: bfloat16 [4096, 14336], P('narrow', 'wide'), may hold values from -0.09375 to 0.09375
- block_codes: int32 [32, 112], P('narrow', 'wide'), may hold values from 0 to 15
- grid: float32 [16], replicated, may hold values from 0.5 to 2
- cotangent: bfloat16 [8192, 14336], P('narrow', 'wide'), may hold values from -6 to 6
Outputs:
- activated: bfloat16 [8192, 14336], P('narrow', 'wide')
- weight_grad: float32 [4096, 14336], P('narrow', 'wide')
- input_grad: bfloat16 [8192, 4096], P('narrow', 'wide')
The draws below stay inside these ranges and needn't reach their ends.
All inputs are finite; a program needn't handle non-finite values.
Results may differ from the reference program's by a relative error of at most 0.017.
Values may be sent and summed in bfloat16 or wider, within the bound.
A program may use at most 128 MiB of HBM per device.

```python
import math
import jax
import jax.numpy as jnp
from jax import lax

D = 4096
FFW = 14336
BLOCK = 128
LEVELS = 16
TOK_DEV = 512
TOKENS = 8192
N_WIDE = 8
N_NARROW = 16


def place_ends(result, rng, low, high):
    extent = result.shape
    index_at = [jax.random.randint(jax.random.fold_in(rng, axis), (), 0, extent[axis]) for axis in range(len(extent))]
    result = result.at[tuple(index_at)].set(low)
    longest = extent.index(max(extent))
    index_at[longest] = (index_at[longest] + 1) % extent[longest]
    return result.at[tuple(index_at)].set(high)


def shard_levels(key, dims, pieces, low, top_value):
    def one(axis_at, blocks):
        heights = jax.random.uniform(jax.random.fold_in(jax.random.fold_in(key, 6), axis_at), (blocks,), jnp.float32, low / len(pieces), top_value / len(pieces))
        return jnp.repeat(jnp.exp(heights), dims[axis_at] // blocks).reshape((-1,) + (1,) * (len(dims) - axis_at - 1))

    loudness = one(*pieces[0])
    for cut in pieces[1:]:
        loudness = loudness * one(*cut)
    return loudness


def bell_draw(stream_key, extent, scale, most, cuts=(), held_as=jnp.bfloat16):
    factor_of = shard_levels(stream_key, extent, cuts, -0.22, 0.18) if cuts else 1.0
    values = jax.random.normal(stream_key, extent, jnp.float32) * scale * factor_of
    return jnp.minimum(jnp.maximum(values, -most), most).astype(held_as)


def setup_inputs(seed: int = 0) -> dict:
    seeds = jax.random.split(jax.random.key(seed), 7)
    return {
        "tokens": bell_draw(seeds[0], (TOKENS, D), 1.0, 6.0, ((0, 16),)),
        "norm_gain": jnp.clip(1.0 + 0.18 * jax.random.normal(seeds[1], (D,), jnp.float32), 0.1, 1.9),
        "coded": bell_draw(seeds[2], (D, FFW), D ** -0.5, 0.09375, ((0, 16), (1, 8))),
        "block_codes": place_ends(jax.random.randint(seeds[3], (D // BLOCK, FFW // BLOCK), 0, LEVELS), jax.random.fold_in(seeds[3], 1), 0, LEVELS - 1).astype(jnp.int32),
        "grid": jnp.clip(jnp.exp(jax.random.uniform(seeds[4], (LEVELS,), jnp.float32, math.log(0.5), math.log(2.0))), 0.5, 2.0),
        "cotangent": bell_draw(seeds[5], (TOKENS, FFW), 1.0, 6.0, ((0, 16), (1, 8))),
    }


def hadamard(size):
    index = jnp.arange(size, dtype=jnp.int32)
    parity = jnp.zeros((size, size), jnp.int32)
    for level in range(size.bit_length() - 1):
        stride = 2 ** level
        parity = parity + index[:, None] // stride % 2 * (index[None, :] // stride % 2)
    return (1 - 2 * (parity % 2)).astype(jnp.bfloat16)

def decode(coded, block_codes, grid):
    nrows, ncols = coded.shape
    rotation = hadamard(BLOCK).astype(jnp.float32)
    onehot = (block_codes[:, :, None] == jnp.arange(grid.shape[0], dtype=jnp.int32)[None, None, :]).astype(jnp.float32)
    block_scale = lax.optimization_barrier(jnp.sum(onehot * grid[None, None, :], axis=-1)) / jnp.sqrt(jnp.float32(BLOCK))
    blocks = coded.reshape(nrows // BLOCK, BLOCK, ncols // BLOCK, BLOCK)

    def one_row(pair):
        piece, scales = pair
        turned = jnp.einsum('ikj,jl->ikl', piece.astype(jnp.float32), rotation)
        return (turned * scales[None, :, None]).reshape(BLOCK, ncols).astype(jnp.bfloat16)
    return lax.map(one_row, (blocks, block_scale)).reshape(nrows, ncols)

def reference(tokens, norm_gain, coded, block_codes, grid, cotangent):
    weight = decode(coded, block_codes, grid)
    inputs = tokens.astype(jnp.float32)
    inv_rms = lax.rsqrt(lax.optimization_barrier(jnp.mean(inputs * inputs, axis=-1, keepdims=True)) + 1e-05)
    normed = (inputs * inv_rms * norm_gain[None, :]).astype(jnp.bfloat16)
    preact = jnp.dot(normed, weight, preferred_element_type=jnp.float32)
    sig = jax.nn.sigmoid(preact)
    activated = (preact * sig).astype(jnp.bfloat16)
    pre_grad = (cotangent.astype(jnp.float32) * sig * (1.0 + preact * (1.0 - sig))).astype(jnp.bfloat16)

    def add_group(group, total):
        rows_n = lax.dynamic_slice_in_dim(normed, group * TOK_DEV, TOK_DEV, 0)
        rows_g = lax.dynamic_slice_in_dim(pre_grad, group * TOK_DEV, TOK_DEV, 0)
        term = jnp.dot(rows_n.T, rows_g, preferred_element_type=jnp.float32)
        return total + term.astype(jnp.bfloat16).astype(jnp.float32)
    weight_grad = lax.fori_loop(0, N_NARROW, add_group, jnp.zeros((D, FFW), jnp.float32))
    width = FFW // N_WIDE

    def add_columns(group, total):
        cols_g = lax.dynamic_slice_in_dim(pre_grad, group * width, width, 1)
        cols_w = lax.dynamic_slice_in_dim(weight, group * width, width, 1)
        term = lax.dot_general(cols_g, cols_w, (((1,), (1,)), ((), ())), preferred_element_type=jnp.float32)
        return total + term.astype(jnp.bfloat16).astype(jnp.float32)
    normed_grad = lax.fori_loop(0, N_WIDE, add_columns, jnp.zeros((TOKENS, D), jnp.float32))
    scaled_grad = normed_grad * norm_gain[None, :]
    row_dot = lax.optimization_barrier(jnp.mean(scaled_grad * inputs, axis=-1, keepdims=True))
    input_grad = (inv_rms * scaled_grad - inputs * inv_rms ** 3 * row_dot).astype(jnp.bfloat16)
    return (activated, weight_grad, input_grad)
```

```python
import jax
import jax.numpy as jnp
from jax import lax
from jax.experimental import pallas as pl
from jax.experimental.pallas import tpu as pltpu
from jax.sharding import PartitionSpec as P

MESH = pl.DeviceIdType.MESH
F32, BF16 = jnp.float32, jnp.bfloat16

D = 4096
TOK = 512
CW = 1792
HALF = 896
BLK = 128
CH = HALF // BLK
CR = 512
R1 = 224
R2 = CR - R1
H1, H2 = R1 // 2, R2 // 2
NB = 4
TB = TOK // NB
XS = D // 4
WS = D // 8


def hadamard():
    both = lax.broadcasted_iota(jnp.int32, (BLK, BLK), 0) & lax.broadcasted_iota(
        jnp.int32, (BLK, BLK), 1
    )
    for shift in (4, 2, 1):
        both = both ^ lax.shift_right_logical(both, shift)
    return (1 - 2 * (both & 1)).astype(F32).astype(BF16)


class Lane:
    def __init__(self, send_sems, recv_sems):
        self.send_sems, self.recv_sems, self.kinds, self.rows = send_sems, recv_sems, {}, {}

    def add(self, name, src, dst, device, land):
        self.rows[name] = len(self.kinds)
        self.kinds[name] = (src, dst, device, land)

    def start(self, name, k):
        src, dst, device, _ = self.kinds[name]
        row = self.rows[name]
        pltpu.make_async_remote_copy(
            src_ref=src(k),
            dst_ref=dst(k),
            send_sem=self.send_sems.at[row, k],
            recv_sem=self.recv_sems.at[row, k],
            device_id=device,
            device_id_type=MESH,
        ).start()

    def arrived(self, name, k):
        _, _, device, land = self.kinds[name]
        row = self.rows[name]
        pltpu.make_async_remote_copy(
            src_ref=land(k),
            dst_ref=land(k),
            send_sem=self.send_sems.at[row, k],
            recv_sem=self.recv_sems.at[row, k],
            device_id=device,
            device_id_type=MESH,
        ).wait_recv()

    def sent(self, name, k):
        src, dst, device, _ = self.kinds[name]
        row = self.rows[name]
        pltpu.make_async_remote_copy(
            src_ref=src(k),
            dst_ref=dst(k),
            send_sem=self.send_sems.at[row, k],
            recv_sem=self.recv_sems.at[row, k],
            device_id=device,
            device_id_type=MESH,
        ).wait_send()

    def drain(self, count):
        @pl.loop(0, count)
        def _(k):
            for name in self.kinds:
                self.sent(name, k)


def kernel(
    tokens, gain, coded, codes, grid, cot,
    act_out, wg_out, ig_out,
    cod, wsib, w, normed, pg, act, g, fin,
    ng, nr, xf, xn, hs, hr, ho, tsl, igv,
    inv, rdacc, rdo, rdr, rdw,
    ry1, rf, rg, rn, rm, ry2,
    loc, act_sem, wg_sem, ig_sem,
    ag_s, ag_r, rs_s, rs_r, sw_s, sw_r, nm_s, nm_r, x_s, x_r, rd_s, rd_r, rw_s, rw_r, ct_s, ct_r,
):
    wi, ni = lax.axis_index("wide"), lax.axis_index("narrow")
    x, yh = wi // 2, wi % 2
    yl, z, c = ni // 8, (ni // 2) % 4, ni % 2
    zp, zm, z2 = (z + 1) % 4, (z + 3) % 4, (z + 2) % 4
    xp, xm, x2 = (x + 1) % 4, (x + 3) % 4, (x + 2) % 4
    yo = 1 - yl
    dev_zp = (wi, (yl * 4 + zp) * 2 + c)
    dev_zm = (wi, (yl * 4 + zm) * 2 + c)
    dev_y = (wi, (yo * 4 + z) * 2 + c)
    dev_c = (wi, (yl * 4 + z) * 2 + (1 - c))
    dev_xp = (xp * 2 + yh, ni)
    dev_xm = (xm * 2 + yh, ni)
    dev_h = (x * 2 + (1 - yh), ni)
    dev_w = [((wi + r) % 8, ni) for r in range(1, 8)]

    def cols(k):
        return pl.ds(pl.multiple_of(k * BLK, BLK), BLK)

    def wide_cols(core, k):
        return pl.ds(pl.multiple_of(core * HALF + k * BLK, BLK), BLK)

    def trows(j, base=0):
        return pl.ds(pl.multiple_of(base + j * TB, TB), TB)

    mine = pl.ds(pl.multiple_of(c * 256, 256), 256)
    other = pl.ds(pl.multiple_of((1 - c) * 256, 256), 256)

    load_cod = pltpu.make_async_copy(coded, cod, loc.at[0])
    load_tok = pltpu.make_async_copy(tokens, ng.at[pl.ds(0, TOK)], loc.at[1])
    load_cot = pltpu.make_async_copy(
        cot.at[:, pl.ds(pl.multiple_of(c * HALF, BLK), HALF)], pg.at[pl.ds(0, TOK)], loc.at[2]
    )
    load_tsl = pltpu.make_async_copy(
        tokens.at[:, pl.ds(pl.multiple_of(wi * WS, BLK), WS)], tsl, loc.at[3]
    )
    load_cod.start()
    load_tok.start()
    load_cot.start()
    load_tsl.start()

    barrier = pltpu.get_barrier_semaphore()
    partners = [dev_zp, dev_zm, dev_y, dev_c, *dev_w]
    for device in partners:
        pl.semaphore_signal(barrier, inc=1, device_id=device, device_id_type=MESH)
    pl.semaphore_wait(barrier, len(partners))

    swap = Lane(sw_s, sw_r)
    swap.add(
        "w",
        lambda k: wsib.at[:, cols(k)],
        lambda k: w.at[yl, z, mine, cols(k)],
        dev_c,
        lambda k: w.at[yl, z, other, cols(k)],
    )
    cts = Lane(ct_s, ct_r)
    cts.add(
        "c",
        lambda k: cot.at[:, pl.ds(pl.multiple_of((1 - c) * HALF, BLK), HALF)],
        lambda k: pg.at[pl.ds(TOK, TOK)],
        dev_c,
        lambda k: pg.at[pl.ds(TOK, TOK)],
    )
    nms = Lane(nm_s, nm_r)
    nms.add(
        "n",
        lambda j: normed.at[trows(j)],
        lambda j: normed.at[trows(j, TOK)],
        dev_c,
        lambda j: normed.at[trows(j, TOK)],
    )

    ag = Lane(ag_s, ag_r)

    def piece(name, device, src_at, land_at, lo, n):
        ag.add(
            name,
            lambda k: w.at[src_at[0], src_at[1], pl.ds(lo, n), cols(k)],
            lambda k: w.at[src_at[0], src_at[1], pl.ds(lo, n), cols(k)],
            device,
            lambda k: w.at[land_at[0], land_at[1], pl.ds(lo, n), cols(k)],
        )

    piece("own_zp", dev_zp, (yl, z), (yl, zm), 0, CR)
    piece("own_zm", dev_zm, (yl, z), (yl, zp), 0, CR)
    piece("own_y", dev_y, (yl, z), (yo, z), 0, CR)
    piece("far_zp", dev_zp, (yl, zm), (yl, z2), 0, CR // 2)
    piece("far_zm", dev_zm, (yl, zp), (yl, z2), CR // 2, CR // 2)
    piece("zm_y", dev_y, (yl, zm), (yo, zm), 0, R1)
    piece("zp_y", dev_y, (yl, zp), (yo, zp), 0, R1)
    piece("y_zp", dev_zp, (yo, z), (yo, zm), R1, R2)
    piece("y_zm", dev_zm, (yo, z), (yo, zp), R1, R2)
    piece("z2_y", dev_y, (yl, z2), (yo, z2), 0, R1)
    piece("yfar_zp", dev_zp, (yo, zm), (yo, z2), R1, H2)
    piece("yfar_zm", dev_zm, (yo, zp), (yo, z2), R1 + H2, H2)

    def ag_a(k):
        swap.arrived("w", k)
        ag.start("own_zp", k)
        ag.start("own_zm", k)
        ag.start("own_y", k)

    def ag_b(k):
        ag.arrived("own_y", k)
        ag.start("y_zp", k)
        ag.start("y_zm", k)
        ag.arrived("own_zp", k)
        ag.start("far_zp", k)
        ag.start("zm_y", k)
        ag.arrived("own_zm", k)
        ag.start("far_zm", k)
        ag.start("zp_y", k)

    def ag_c(k):
        ag.arrived("far_zp", k)
        ag.start("z2_y", k)
        ag.arrived("y_zp", k)
        ag.start("yfar_zp", k)
        ag.arrived("y_zm", k)
        ag.start("yfar_zm", k)

    def ag_d(k):
        for name in ("far_zm", "zm_y", "zp_y", "z2_y", "yfar_zp", "yfar_zm"):
            ag.arrived(name, k)

    rs = Lane(rs_s, rs_r)
    rs.add("a_y", lambda k: g.at[yo, :, pl.ds(0, R1), cols(k)], lambda k: ry1.at[k], dev_y,
           lambda k: ry1.at[k])
    rs.add("a_zp", lambda k: g.at[:, z2, pl.ds(R1, H2), cols(k)], lambda k: rf.at[0, k], dev_zp,
           lambda k: rf.at[0, k])
    rs.add("a_zm", lambda k: g.at[:, z2, pl.ds(R1 + H2, H2), cols(k)], lambda k: rf.at[1, k],
           dev_zm, lambda k: rf.at[1, k])
    rs.add("b1_zp", lambda k: g.at[yl, z2, pl.ds(0, H1), cols(k)], lambda k: rg.at[0, k], dev_zp,
           lambda k: rg.at[0, k])
    rs.add("b1_zm", lambda k: g.at[yl, z2, pl.ds(H1, H1), cols(k)], lambda k: rg.at[1, k], dev_zm,
           lambda k: rg.at[1, k])
    rs.add("b2_zp", lambda k: g.at[:, zp, pl.ds(R1, R2), cols(k)], lambda k: rn.at[0, k], dev_zp,
           lambda k: rn.at[0, k])
    rs.add("b2_zm", lambda k: g.at[:, zm, pl.ds(R1, R2), cols(k)], lambda k: rn.at[1, k], dev_zm,
           lambda k: rn.at[1, k])
    rs.add("c_zp", lambda k: g.at[yl, zp, pl.ds(0, R1), cols(k)], lambda k: rm.at[0, k], dev_zp,
           lambda k: rm.at[0, k])
    rs.add("c_zm", lambda k: g.at[yl, zm, pl.ds(0, R1), cols(k)], lambda k: rm.at[1, k], dev_zm,
           lambda k: rm.at[1, k])
    rs.add("c_y", lambda k: g.at[yo, z, pl.ds(R1, R2), cols(k)], lambda k: ry2.at[k], dev_y,
           lambda k: ry2.at[k])

    def plus(first, *rest):
        total = first.astype(F32)
        for term in rest:
            total = total + term.astype(F32)
        return total

    def add_into(at, *terms):
        g[at] = plus(g[at], *terms).astype(BF16)

    def rs_a(k):
        rs.start("a_y", k)
        rs.start("a_zp", k)
        rs.start("a_zm", k)

    def rs_b(k):
        rs.arrived("a_zp", k)
        add_into((slice(None), zp, pl.ds(R1, H2), cols(k)), rf[0, k])
        rs.start("b2_zp", k)
        rs.arrived("a_zm", k)
        add_into((slice(None), zm, pl.ds(R1 + H2, H2), cols(k)), rf[1, k])
        rs.start("b2_zm", k)
        rs.arrived("a_y", k)
        add_into((yl, slice(None), pl.ds(0, R1), cols(k)), ry1[k])
        rs.start("b1_zp", k)
        rs.start("b1_zm", k)

    def rs_c(k):
        rs.arrived("b2_zp", k)
        rs.arrived("b2_zm", k)
        add_into((slice(None), z, pl.ds(R1, R2), cols(k)), rn[0, k], rn[1, k])
        rs.start("c_y", k)
        rs.arrived("b1_zp", k)
        add_into((yl, zp, pl.ds(0, H1), cols(k)), rg[0, k])
        rs.start("c_zp", k)
        rs.arrived("b1_zm", k)
        add_into((yl, zm, pl.ds(H1, H1), cols(k)), rg[1, k])
        rs.start("c_zm", k)

    def wg_local(k):
        return pltpu.make_async_copy(
            fin.at[mine, cols(k)], wg_out.at[:, wide_cols(c, k)], wg_sem.at[0, k]
        )

    def wg_remote(k, landed=False):
        target = wg_out.at[:, wide_cols((1 - c) if landed else c, k)]
        return pltpu.make_async_remote_copy(
            src_ref=fin.at[other, cols(k)],
            dst_ref=target,
            send_sem=wg_sem.at[1, k],
            recv_sem=wg_sem.at[2, k],
            device_id=dev_c,
            device_id_type=MESH,
        )

    def rs_d(k):
        rs.arrived("c_zp", k)
        rs.arrived("c_zm", k)
        fin[pl.ds(0, R1), cols(k)] = plus(g[yl, z, pl.ds(0, R1), cols(k)], rm[0, k], rm[1, k])
        rs.arrived("c_y", k)
        fin[pl.ds(R1, R2), cols(k)] = plus(g[yl, z, pl.ds(R1, R2), cols(k)], ry2[k])
        wg_local(k).start()
        wg_remote(k).start()

    def act_local(k):
        return pltpu.make_async_copy(
            act.at[pl.ds(0, TOK), cols(k)], act_out.at[:, wide_cols(c, k)], act_sem.at[0, k]
        )

    def act_remote(k, landed=False):
        return pltpu.make_async_remote_copy(
            src_ref=act.at[pl.ds(TOK, TOK), cols(k)],
            dst_ref=act_out.at[:, wide_cols((1 - c) if landed else c, k)],
            send_sem=act_sem.at[1, k],
            recv_sem=act_sem.at[2, k],
            device_id=dev_c,
            device_id_type=MESH,
        )

    def compute(k):
        @pl.loop(0, 4)
        def _(t):
            rows = pl.ds(pl.multiple_of(t * 256, 256), 256)
            weight = w[:, :, :, cols(k)].reshape(D, BLK)
            preact = jnp.dot(normed[rows], weight, preferred_element_type=F32)
            sig = 1.0 / (1.0 + jnp.exp(-preact))
            act[rows, cols(k)] = (preact * sig).astype(BF16)
            grad = (pg[rows, cols(k)].astype(F32) * sig * (1.0 + preact * (1.0 - sig))).astype(BF16)
            pg[rows, cols(k)] = grad
            rdacc[rows] += preact * grad.astype(F32)

        act_local(k).start()
        act_remote(k).start()
        turned = pg[:, cols(k)].T
        for q in range(8):
            part = jnp.dot(turned, normed[:, q * CR : (q + 1) * CR], preferred_element_type=F32)
            g[q // 4, q % 4, :, cols(k)] = part.T.astype(BF16)

    xs = Lane(x_s, x_r)

    def span(start, n):
        return pl.ds(pl.multiple_of(start, BLK), n)

    xs.add("sib", lambda j: ng.at[trows(j, TOK)], lambda j: nr.at[trows(j)], dev_c,
           lambda j: nr.at[trows(j)])
    xs.add("far_p", lambda j: ng.at[trows(j), span(x2 * XS, WS)], lambda j: xf.at[0, trows(j)],
           dev_xp, lambda j: xf.at[0, trows(j)])
    xs.add("far_m", lambda j: ng.at[trows(j), span(x2 * XS + WS, WS)], lambda j: xf.at[1, trows(j)],
           dev_xm, lambda j: xf.at[1, trows(j)])
    xs.add("near_p", lambda j: ng.at[trows(j), span(xp * XS, XS)], lambda j: xn.at[0, trows(j)],
           dev_xp, lambda j: xn.at[0, trows(j)])
    xs.add("near_m", lambda j: ng.at[trows(j), span(xm * XS, XS)], lambda j: xn.at[1, trows(j)],
           dev_xm, lambda j: xn.at[1, trows(j)])
    xs.add("h", lambda j: hs.at[trows(j)], lambda j: hr.at[trows(j)], dev_h,
           lambda j: hr.at[trows(j)])

    def ng_p(j):
        grads = jnp.concatenate([pg[trows(j)], pg[trows(j, TOK)]], axis=0)
        for q in range(8):
            part = lax.dot_general(
                grads, w[q // 4, q % 4], (((1,), (1,)), ((), ())), preferred_element_type=F32
            ).astype(BF16)
            ng[trows(j), q * CR : (q + 1) * CR] = part[:TB]
            ng[trows(j, TOK), q * CR : (q + 1) * CR] = part[TB:]
        xs.start("sib", j)

    def ng_q(j):
        xs.arrived("sib", j)
        ng[trows(j)] = plus(ng[trows(j)], nr[trows(j)]).astype(BF16)
        xs.start("far_p", j)
        xs.start("far_m", j)

    def ng_r(j):
        xs.arrived("far_p", j)
        at = (trows(j), span(xp * XS, WS))
        ng[at] = plus(ng[at], xf[0, trows(j)]).astype(BF16)
        xs.start("near_p", j)
        xs.arrived("far_m", j)
        at = (trows(j), span(xm * XS + WS, WS))
        ng[at] = plus(ng[at], xf[1, trows(j)]).astype(BF16)
        xs.start("near_m", j)

    def ng_u(j):
        xs.arrived("near_p", j)
        xs.arrived("near_m", j)
        theirs, ours = span((1 - yh) * WS, WS), span(yh * WS, WS)
        base = x * XS
        hs[trows(j)] = plus(
            ng[trows(j), span(base + (1 - yh) * WS, WS)],
            xn[0, trows(j), theirs],
            xn[1, trows(j), theirs],
        ).astype(BF16)
        xs.start("h", j)
        ho[trows(j)] = plus(
            ng[trows(j), span(base + yh * WS, WS)], xn[0, trows(j), ours], xn[1, trows(j), ours]
        )

    def ig_copy(j):
        return pltpu.make_async_copy(igv.at[trows(j)], ig_out.at[trows(j)], ig_sem.at[j])

    def ng_v(j):
        xs.arrived("h", j)
        scaled = plus(ho[trows(j)], hr[trows(j)]) * gain[:, span(wi * WS, WS)]
        scale = inv[trows(j)][:, :1]
        dots = rdacc[trows(j)][:, :1]
        igv[trows(j)] = (scale * scaled - tsl[trows(j)].astype(F32) * (scale * scale) * dots).astype(
            BF16
        )
        ig_copy(j).start()

    rds = Lane(rd_s, rd_r)
    rds.add("s", lambda k: rdo.at[1], lambda k: rdr, dev_c, lambda k: rdr)
    rws = Lane(rw_s, rw_r)
    for r in range(7):
        rws.add(str(r), lambda k: rdo.at[0], lambda k, r=r: rdw.at[r], dev_w[r],
                lambda k, r=r: rdw.at[r])

    def rd_1():
        ones = jnp.ones((8, BLK), F32)
        for half in range(2):
            rdo[half] = lax.dot_general(
                ones,
                rdacc[half * TOK : (half + 1) * TOK],
                (((1,), (1,)), ((), ())),
                precision=lax.Precision.HIGHEST,
                preferred_element_type=F32,
            )
        rds.start("s", 0)

    def rd_2():
        rds.arrived("s", 0)
        rdo[0] = rdo[0] + rdr[...]
        for r in range(7):
            rws.start(str(r), 0)

    def rd_3():
        for r in range(7):
            rws.arrived(str(r), 0)
        total = rdo[0]
        for r in range(7):
            total = total + rdw[r]
        rdacc[pl.ds(0, TOK)] = jnp.broadcast_to((total / D).T[:, :1], (TOK, BLK))

    cts.start("c", 0)
    rotation = hadamard()
    load_cod.wait()

    def decoded(core, k):
        at = wide_cols(core, k)
        turned = jnp.dot(cod[:, at], rotation, preferred_element_type=F32)
        block = core * CH + k
        norm = 1.0 / (BLK**0.5)
        top = turned[:BLK] * (grid[codes[0, block]] * norm)
        low = turned[BLK:] * (grid[codes[1, block]] * norm)
        return jnp.concatenate([top, low], axis=0).astype(BF16)

    @pl.loop(0, CH)
    def _(k):
        wsib[:, cols(k)] = decoded(1 - c, k)
        swap.start("w", k)
        w[yl, z, mine, cols(k)] = decoded(c, k)

    ag_a(0)
    ag_a(1)
    rdacc[...] = jnp.zeros_like(rdacc)
    load_tok.wait()

    @pl.loop(0, NB)
    def _(j):
        @pl.loop(0, TB // 32)
        def _(i):
            rows = pl.ds(pl.multiple_of(j * TB + i * 32, 32), 32)
            values = ng[rows].astype(F32)
            scale = lax.rsqrt(jnp.sum(values * values, axis=-1, keepdims=True) * (1.0 / D) + 1e-5)
            inv[rows] = jnp.broadcast_to(scale, (32, BLK))
            normed[rows] = (values * scale * gain[...]).astype(BF16)

        nms.start("n", j)

    @pl.loop(0, CH + 2)
    def _(s):
        @pl.when(s + 2 < CH)
        def _():
            ag_a(s + 2)

        @pl.when(s < CH)
        def _():
            ag_b(s)

        @pl.when((s >= 1) & (s < CH + 1))
        def _():
            ag_c(s - 1)

        @pl.when(s >= CH)
        def _():
            rs_a(s - CH)

        @pl.when(s == 2)
        def _():
            load_cot.wait()
            cts.arrived("c", 0)
            for j in range(NB):
                nms.arrived("n", j)

        @pl.when(s >= 2)
        def _():
            ag_d(s - 2)
            compute(s - 2)

    rd_1()

    @pl.loop(0, CH + 2)
    def _(t):
        @pl.when(t + 2 < CH)
        def _():
            rs_a(t + 2)

        @pl.when(t < NB)
        def _():
            ng_p(t)

        @pl.when(t < CH)
        def _():
            rs_b(t)

        @pl.when(t < NB)
        def _():
            ng_q(t)

        @pl.when((t >= 1) & (t < CH + 1))
        def _():
            rs_c(t - 1)

        @pl.when(t == 1)
        def _():
            rd_2()

        @pl.when((t >= 2) & (t < NB + 2))
        def _():
            ng_r(t - 2)

        @pl.when(t >= 2)
        def _():
            rs_d(t - 2)

        @pl.when(t == 3)
        def _():
            load_tsl.wait()
            rd_3()

        @pl.when((t >= 4) & (t < NB + 4))
        def _():
            ng_u(t - 4)

        @pl.when((t >= 5) & (t < NB + 5))
        def _():
            ng_v(t - 5)

    swap.drain(CH)
    ag.drain(CH)
    rs.drain(CH)
    nms.drain(NB)
    xs.drain(NB)
    cts.sent("c", 0)
    rds.sent("s", 0)
    for r in range(7):
        rws.sent(str(r), 0)

    @pl.loop(0, CH)
    def _(k):
        act_local(k).wait()
        act_remote(k).wait_send()
        act_remote(k, True).wait_recv()
        wg_local(k).wait()
        wg_remote(k).wait_send()
        wg_remote(k, True).wait_recv()

    @pl.loop(0, NB)
    def _(j):
        ig_copy(j).wait()


def per_device(tokens, norm_gain, coded, block_codes, grid, cotangent):
    anywhere = pl.BlockSpec(memory_space=pl.ANY)
    vmem = pl.BlockSpec(memory_space=pltpu.VMEM)
    smem = pl.BlockSpec(memory_space=pltpu.SMEM)
    sem = pltpu.SemaphoreType.DMA
    return pl.pallas_call(
        kernel,
        out_shape=(
            jax.ShapeDtypeStruct((TOK, CW), BF16),
            jax.ShapeDtypeStruct((D // 16, CW), F32),
            jax.ShapeDtypeStruct((TOK, WS), BF16),
        ),
        in_specs=[anywhere, vmem, anywhere, smem, smem, anywhere],
        out_specs=(anywhere, anywhere, anywhere),
        scratch_shapes=[
            pltpu.VMEM((256, CW), BF16),
            pltpu.VMEM((256, HALF), BF16),
            pltpu.VMEM((2, 4, CR, HALF), BF16),
            pltpu.VMEM((2 * TOK, D), BF16),
            pltpu.VMEM((2 * TOK, HALF), BF16),
            pltpu.VMEM((2 * TOK, HALF), BF16),
            pltpu.VMEM((2, 4, CR, HALF), BF16),
            pltpu.VMEM((CR, HALF), F32),
            pltpu.VMEM((2 * TOK, D), BF16),
            pltpu.VMEM((TOK, D), BF16),
            pltpu.VMEM((2, TOK, WS), BF16),
            pltpu.VMEM((2, TOK, XS), BF16),
            pltpu.VMEM((TOK, WS), BF16),
            pltpu.VMEM((TOK, WS), BF16),
            pltpu.VMEM((TOK, WS), F32),
            pltpu.VMEM((TOK, WS), BF16),
            pltpu.VMEM((TOK, WS), BF16),
            pltpu.VMEM((TOK, BLK), F32),
            pltpu.VMEM((2 * TOK, BLK), F32),
            pltpu.VMEM((2, 8, TOK), F32),
            pltpu.VMEM((8, TOK), F32),
            pltpu.VMEM((7, 8, TOK), F32),
            pltpu.VMEM((CH, 4, R1, BLK), BF16),
            pltpu.VMEM((2, CH, 2, H2, BLK), BF16),
            pltpu.VMEM((2, CH, H1, BLK), BF16),
            pltpu.VMEM((2, CH, 2, R2, BLK), BF16),
            pltpu.VMEM((2, CH, R1, BLK), BF16),
            pltpu.VMEM((CH, R2, BLK), BF16),
            sem((4,)), sem((3, CH)), sem((3, CH)), sem((NB,)),
            sem((12, CH)), sem((12, CH)), sem((10, CH)), sem((10, CH)),
            sem((1, CH)), sem((1, CH)), sem((1, NB)), sem((1, NB)),
            sem((6, NB)), sem((6, NB)), sem((1, 1)), sem((1, 1)),
            sem((7, 1)), sem((7, 1)), sem((1, 1)), sem((1, 1)),
        ],
        compiler_params=pltpu.CompilerParams(
            collective_id=0, has_side_effects=True, vmem_limit_bytes=63 << 20
        ),
        cost_estimate=pl.CostEstimate(
            flops=6 * TOK * D * CW, bytes_accessed=40 << 20, transcendentals=TOK * CW
        ),
    )(tokens, norm_gain.reshape(1, D), coded, block_codes, grid, cotangent)


def solution(mesh):
    placed = (
        P("narrow", None), P(), P("narrow", "wide"), P("narrow", "wide"), P(), P("narrow", "wide"),
    )
    return jax.shard_map(
        per_device,
        mesh=mesh,
        in_specs=placed,
        out_specs=(P("narrow", "wide"), P("narrow", "wide"), P("narrow", "wide")),
        check_vma=False,
    )
```

```python
import jax
import jax.numpy as jnp
from jax import lax
from jax.experimental import pallas as pl
from jax.experimental.pallas import tpu as pltpu
from jax.sharding import PartitionSpec as P

MESH = pl.DeviceIdType.MESH
F32, BF16 = jnp.float32, jnp.bfloat16

D = 4096
TOK = 512
CW = 1792
HALF = 896
BLK = 128
CH = HALF // BLK
CR = 512
G1 = 224
G2, GH = CR - G1, (CR - G1) // 2
R1 = 160
R2 = CR - R1
H1, H2 = R1 // 2, R2 // 2
KP = 4 * BLK
NB = 8
TB = TOK // NB
XS = D // 4
WS = D // 8

LA, LC, LD = 1, 1, 2
RC, RD = 1, 3
NR, NU, NV = 2, 4, 5
ER, EU = 2, 2
STEPS = CH - 1 + LD + max(CH + RD, NV + NB // EU)


def hadamard():
    both = lax.broadcasted_iota(jnp.int32, (BLK, BLK), 0) & lax.broadcasted_iota(
        jnp.int32, (BLK, BLK), 1
    )
    for shift in (4, 2, 1):
        both = both ^ lax.shift_right_logical(both, shift)
    return (1 - 2 * (both & 1)).astype(F32).astype(BF16)


class Lane:
    def __init__(self, send_sems, recv_sems):
        self.send_sems, self.recv_sems, self.kinds, self.rows = send_sems, recv_sems, {}, {}

    def add(self, name, src, dst, device, land, whole):
        self.rows[name] = len(self.kinds)
        self.kinds[name] = (src, dst, device, land, whole)

    def copy(self, name, k, src, dst):
        row = self.rows[name]
        return pltpu.make_async_remote_copy(
            src_ref=src,
            dst_ref=dst,
            send_sem=self.send_sems.at[row],
            recv_sem=self.recv_sems.at[row, k],
            device_id=self.kinds[name][2],
            device_id_type=MESH,
        )

    def start(self, name, k):
        src, dst, _, _, _ = self.kinds[name]
        self.copy(name, k, src(k), dst(k)).start()

    def arrived(self, name, k):
        land = self.kinds[name][3]
        self.copy(name, k, land(k), land(k)).wait_recv()

    def drain(self):
        for name, (_, _, _, _, whole) in self.kinds.items():
            self.copy(name, 0, whole, whole).wait_send()


def kernel(
    tokens, gain, coded, codes, grid, cot,
    act_out, wg_out, ig_out,
    cod, wsib, w, normed, pg, act, g, fin,
    ng, nr, xf, xn, hs, hr, ho, tsl, igv,
    inv, rdacc, rdo, rdr, rdw,
    ry1, rf, rg, rn, rm, ry2,
    loc, act_sem, wg_sem, ig_sem,
    ag_s, ag_r, rs_s, rs_r, si_s, si_r, sw_s, sw_r, nm_s, nm_r, x_s, x_r, rd_s, rd_r, rw_s, rw_r, ct_s, ct_r,
):
    wi, ni = lax.axis_index("wide"), lax.axis_index("narrow")
    x, yh = wi // 2, wi % 2
    yl, z, c = ni // 8, (ni // 2) % 4, ni % 2
    zp, zm, z2 = (z + 1) % 4, (z + 3) % 4, (z + 2) % 4
    xp, xm, x2 = (x + 1) % 4, (x + 3) % 4, (x + 2) % 4
    yo = 1 - yl
    dev_zp = (wi, (yl * 4 + zp) * 2 + c)
    dev_zm = (wi, (yl * 4 + zm) * 2 + c)
    dev_y = (wi, (yo * 4 + z) * 2 + c)
    dev_c = (wi, (yl * 4 + z) * 2 + (1 - c))
    dev_xp = (xp * 2 + yh, ni)
    dev_xm = (xm * 2 + yh, ni)
    dev_h = (x * 2 + (1 - yh), ni)
    dev_w = [((wi + r) % 8, ni) for r in range(1, 8)]

    def cols(k):
        return pl.ds(pl.multiple_of(k * BLK, BLK), BLK)

    def wide_cols(core, k):
        return pl.ds(pl.multiple_of(core * HALF + k * BLK, BLK), BLK)

    def trows(j, base=0):
        return pl.ds(pl.multiple_of(base + j * TB, TB), TB)

    mine = pl.ds(pl.multiple_of(c * 256, 256), 256)
    other = pl.ds(pl.multiple_of((1 - c) * 256, 256), 256)

    load_cod = pltpu.make_async_copy(coded, cod, loc.at[0])
    load_tok = pltpu.make_async_copy(tokens, ng.at[pl.ds(0, TOK)], loc.at[1])
    load_cot = pltpu.make_async_copy(
        cot.at[:, pl.ds(pl.multiple_of(c * HALF, BLK), HALF)], pg.at[pl.ds(0, TOK)], loc.at[2]
    )
    load_tsl = pltpu.make_async_copy(
        tokens.at[:, pl.ds(pl.multiple_of(wi * WS, BLK), WS)], tsl, loc.at[3]
    )
    load_cod.start()
    barrier = pltpu.get_barrier_semaphore()
    partners = [dev_zp, dev_zm, dev_y, dev_c, *dev_w]
    for device in partners:
        pl.semaphore_signal(barrier, inc=1, device_id=device, device_id_type=MESH)
    load_tok.start()
    load_cot.start()
    load_tsl.start()
    load_cod.wait()
    pl.semaphore_wait(barrier, len(partners))

    swap = Lane(sw_s, sw_r)
    swap.add(
        "w",
        lambda k: wsib.at[:, cols(k)],
        lambda k: w.at[yl, z, mine, cols(k)],
        dev_c,
        lambda k: w.at[yl, z, other, cols(k)],
        wsib,
    )
    cts = Lane(ct_s, ct_r)
    cts.add(
        "c",
        lambda k: cot.at[:, pl.ds(pl.multiple_of((1 - c) * HALF, BLK), HALF)],
        lambda k: pg.at[pl.ds(TOK, TOK)],
        dev_c,
        lambda k: pg.at[pl.ds(TOK, TOK)],
        pg.at[pl.ds(TOK, TOK)],
    )
    nms = Lane(nm_s, nm_r)
    nms.add(
        "n",
        lambda j: normed.at[trows(j)],
        lambda j: normed.at[trows(j, TOK)],
        dev_c,
        lambda j: normed.at[trows(j, TOK)],
        normed.at[pl.ds(TOK, TOK)],
    )

    ag = Lane(ag_s, ag_r)

    def piece(name, device, src_at, land_at, lo, n):
        ag.add(
            name,
            lambda k: w.at[src_at[0], src_at[1], pl.ds(lo, n), cols(k)],
            lambda k: w.at[src_at[0], src_at[1], pl.ds(lo, n), cols(k)],
            device,
            lambda k: w.at[land_at[0], land_at[1], pl.ds(lo, n), cols(k)],
            w.at[src_at[0], src_at[1], pl.ds(lo, n)],
        )

    piece("own_zp", dev_zp, (yl, z), (yl, zm), 0, CR)
    piece("own_zm", dev_zm, (yl, z), (yl, zp), 0, CR)
    piece("own_y", dev_y, (yl, z), (yo, z), 0, CR)
    piece("far_zp", dev_zp, (yl, zm), (yl, z2), 0, CR // 2)
    piece("far_zm", dev_zm, (yl, zp), (yl, z2), CR // 2, CR // 2)
    piece("zm_y", dev_y, (yl, zm), (yo, zm), 0, G1)
    piece("zp_y", dev_y, (yl, zp), (yo, zp), 0, G1)
    piece("y_zp", dev_zp, (yo, z), (yo, zm), G1, G2)
    piece("y_zm", dev_zm, (yo, z), (yo, zp), G1, G2)
    piece("z2_y", dev_y, (yl, z2), (yo, z2), 0, G1)
    piece("yfar_zp", dev_zp, (yo, zm), (yo, z2), G1, GH)
    piece("yfar_zm", dev_zm, (yo, zp), (yo, z2), G1 + GH, GH)

    def ag_a(k):
        swap.arrived("w", k)
        ag.start("own_zp", k)
        ag.start("own_zm", k)
        ag.start("own_y", k)

    def ag_b(k):
        ag.arrived("own_y", k)
        ag.start("y_zp", k)
        ag.start("y_zm", k)
        ag.arrived("own_zp", k)
        ag.start("far_zp", k)
        ag.start("zm_y", k)
        ag.arrived("own_zm", k)
        ag.start("far_zm", k)
        ag.start("zp_y", k)

    def ag_c(k):
        ag.arrived("far_zp", k)
        ag.start("z2_y", k)
        ag.arrived("y_zp", k)
        ag.start("yfar_zp", k)
        ag.arrived("y_zm", k)
        ag.start("yfar_zm", k)

    def ag_d(k):
        for name in ("far_zm", "zm_y", "zp_y", "z2_y", "yfar_zp", "yfar_zm"):
            ag.arrived(name, k)

    rs = Lane(rs_s, rs_r)
    rs.add("a_y", lambda k: g.at[yo, :, pl.ds(0, R1), cols(k)], lambda k: ry1.at[k], dev_y,
           lambda k: ry1.at[k], g.at[yo, :, pl.ds(0, R1)])
    rs.add("a_zp", lambda k: g.at[:, z2, pl.ds(R1, H2), cols(k)], lambda k: rf.at[0, k], dev_zp,
           lambda k: rf.at[0, k], g.at[:, z2, pl.ds(R1, H2)])
    rs.add("a_zm", lambda k: g.at[:, z2, pl.ds(R1 + H2, H2), cols(k)], lambda k: rf.at[1, k],
           dev_zm, lambda k: rf.at[1, k], g.at[:, z2, pl.ds(R1 + H2, H2)])
    rs.add("b1_zp", lambda k: g.at[yl, z2, pl.ds(0, H1), cols(k)], lambda k: rg.at[0, k], dev_zp,
           lambda k: rg.at[0, k], g.at[yl, z2, pl.ds(0, H1)])
    rs.add("b1_zm", lambda k: g.at[yl, z2, pl.ds(H1, H1), cols(k)], lambda k: rg.at[1, k], dev_zm,
           lambda k: rg.at[1, k], g.at[yl, z2, pl.ds(H1, H1)])
    rs.add("b2_zp", lambda k: g.at[:, zp, pl.ds(R1, R2), cols(k)], lambda k: rn.at[0, k], dev_zp,
           lambda k: rn.at[0, k], g.at[:, zp, pl.ds(R1, R2)])
    rs.add("b2_zm", lambda k: g.at[:, zm, pl.ds(R1, R2), cols(k)], lambda k: rn.at[1, k], dev_zm,
           lambda k: rn.at[1, k], g.at[:, zm, pl.ds(R1, R2)])
    rs.add("c_zp", lambda k: g.at[yl, zp, pl.ds(0, R1), cols(k)], lambda k: rm.at[0, k], dev_zp,
           lambda k: rm.at[0, k], g.at[yl, zp, pl.ds(0, R1)])
    rs.add("c_zm", lambda k: g.at[yl, zm, pl.ds(0, R1), cols(k)], lambda k: rm.at[1, k], dev_zm,
           lambda k: rm.at[1, k], g.at[yl, zm, pl.ds(0, R1)])
    rs.add("c_y", lambda k: g.at[yo, z, pl.ds(R1, R2), cols(k)], lambda k: ry2.at[k], dev_y,
           lambda k: ry2.at[k], g.at[yo, z, pl.ds(R1, R2)])

    def plus(first, *rest):
        total = first.astype(F32)
        for term in rest:
            total = total + term.astype(F32)
        return total

    def add_into(at, *terms):
        total = g[at]
        for term in terms:
            total = total + term
        g[at] = total

    def rs_a(k):
        rs.start("a_y", k)
        rs.start("a_zp", k)
        rs.start("a_zm", k)

    def rs_b(k):
        rs.arrived("a_zp", k)
        add_into((slice(None), zp, pl.ds(R1, H2), cols(k)), rf[0, k])
        rs.start("b2_zp", k)
        rs.arrived("a_zm", k)
        add_into((slice(None), zm, pl.ds(R1 + H2, H2), cols(k)), rf[1, k])
        rs.start("b2_zm", k)
        rs.arrived("a_y", k)
        add_into((yl, slice(None), pl.ds(0, R1), cols(k)), ry1[k])
        rs.start("b1_zp", k)
        rs.start("b1_zm", k)

    def rs_c(k):
        rs.arrived("b2_zp", k)
        rs.arrived("b2_zm", k)
        add_into((slice(None), z, pl.ds(R1, R2), cols(k)), rn[0, k], rn[1, k])
        rs.start("c_y", k)
        rs.arrived("b1_zp", k)
        add_into((yl, zp, pl.ds(0, H1), cols(k)), rg[0, k])
        rs.start("c_zp", k)
        rs.arrived("b1_zm", k)
        add_into((yl, zm, pl.ds(H1, H1), cols(k)), rg[1, k])
        rs.start("c_zm", k)

    def wg_local(k):
        return pltpu.make_async_copy(
            fin.at[mine, cols(k)], wg_out.at[:, wide_cols(c, k)], wg_sem.at[0, k]
        )

    def wg_remote(k, landed=False):
        target = wg_out.at[:, wide_cols((1 - c) if landed else c, k)]
        return pltpu.make_async_remote_copy(
            src_ref=fin.at[other, cols(k)],
            dst_ref=target,
            send_sem=wg_sem.at[1, k],
            recv_sem=wg_sem.at[2, k],
            device_id=dev_c,
            device_id_type=MESH,
        )

    def rs_d(k):
        rs.arrived("c_zp", k)
        rs.arrived("c_zm", k)
        fin[pl.ds(0, R1), cols(k)] = plus(g[yl, z, pl.ds(0, R1), cols(k)], rm[0, k], rm[1, k])
        rs.arrived("c_y", k)
        fin[pl.ds(R1, R2), cols(k)] = plus(g[yl, z, pl.ds(R1, R2), cols(k)], ry2[k])
        wg_local(k).start()
        wg_remote(k).start()

    def act_local(k):
        return pltpu.make_async_copy(
            act.at[pl.ds(0, TOK), cols(k)], act_out.at[:, wide_cols(c, k)], act_sem.at[0, k]
        )

    def act_remote(k, landed=False):
        return pltpu.make_async_remote_copy(
            src_ref=act.at[pl.ds(TOK, TOK), cols(k)],
            dst_ref=act_out.at[:, wide_cols((1 - c) if landed else c, k)],
            send_sem=act_sem.at[1, k],
            recv_sem=act_sem.at[2, k],
            device_id=dev_c,
            device_id_type=MESH,
        )

    def forward(k, count):
        at = pl.ds(pl.multiple_of(k * BLK, BLK), count * BLK)

        @pl.loop(0, 4)
        def _(t):
            rows = pl.ds(pl.multiple_of(t * 256, 256), 256)
            weight = w[:, :, :, at].reshape(D, count * BLK)
            preact = jnp.dot(normed[rows], weight, preferred_element_type=F32)
            sig = 1.0 / (1.0 + jnp.exp(-preact))
            act[rows, at] = (preact * sig).astype(BF16)
            grad = (pg[rows, at].astype(F32) * sig * (1.0 + preact * (1.0 - sig))).astype(BF16)
            pg[rows, at] = grad
            dots = preact * grad.astype(F32)
            for i in range(count):
                rdacc[rows] += dots[:, i * BLK : (i + 1) * BLK]

        for i in range(count):
            act_local(k + i).start()
            act_remote(k + i).start()

    def weight_part(k):
        turned = pg[:, cols(k)].T
        for q in range(8):
            part = jnp.dot(turned, normed[:, q * CR : (q + 1) * CR], preferred_element_type=F32)
            g[q // 4, q % 4, :, cols(k)] = part.T.astype(BF16)

    xs = Lane(x_s, x_r)

    def span(start, n):
        return pl.ds(pl.multiple_of(start, BLK), n)

    xs.add("far_p", lambda j: ng.at[trows(j), span(x2 * XS, WS)], lambda j: xf.at[0, trows(j)],
           dev_xp, lambda j: xf.at[0, trows(j)], ng.at[pl.ds(0, TOK), span(0, WS)])
    xs.add("far_m", lambda j: ng.at[trows(j), span(x2 * XS + WS, WS)], lambda j: xf.at[1, trows(j)],
           dev_xm, lambda j: xf.at[1, trows(j)], ng.at[pl.ds(0, TOK), span(0, WS)])
    xs.add("near_p", lambda j: ng.at[trows(j), span(xp * XS, XS)], lambda j: xn.at[0, trows(j)],
           dev_xp, lambda j: xn.at[0, trows(j)], ng.at[pl.ds(0, TOK), span(0, XS)])
    xs.add("near_m", lambda j: ng.at[trows(j), span(xm * XS, XS)], lambda j: xn.at[1, trows(j)],
           dev_xm, lambda j: xn.at[1, trows(j)], ng.at[pl.ds(0, TOK), span(0, XS)])
    xs.add("h", lambda j: hs.at[trows(j)], lambda j: hr.at[trows(j)], dev_h,
           lambda j: hr.at[trows(j)], hs)

    def quarter(i):
        m, n = i // 2, i % 2
        return (x + 2 - n + m * (1 - 2 * n)) % 4

    sib = Lane(si_s, si_r)
    sib.add(
        "s",
        lambda i: ng.at[pl.ds(TOK, TOK), span(quarter(i) * XS, XS)],
        lambda i: nr.at[:, span(quarter(i) * XS, XS)],
        dev_c,
        lambda i: nr.at[:, span(quarter(i) * XS, XS)],
        nr,
    )

    def grads_times_weight(i, t, lo, n, first):
        rows = pl.ds(pl.multiple_of((1 - t) * TOK, TOK), TOK)
        for h in range(2):
            block = quarter(i) * 2 + h
            part = lax.dot_general(
                pg[rows, lo : lo + n],
                w[block // 4, block % 4, :, lo : lo + n],
                (((1,), (1,)), ((), ())),
                preferred_element_type=F32,
            )
            at = (rows, span(block * CR, CR))
            ng[at] = part.astype(BF16) if first else plus(part, ng[at]).astype(BF16)

    def ng_first(i):
        @pl.loop(0, 2)
        def _(t):
            grads_times_weight(i, t, 0, KP, True)

    def ng_p(i):
        @pl.loop(0, 2)
        def _(t):
            grads_times_weight(i, t, KP, HALF - KP, False)

            @pl.when(t == 0)
            def _():
                sib.start("s", i)

    def ng_q():
        sib.arrived("s", 0)

        @pl.loop(0, NB)
        def _(j):
            at = (trows(j), span(x2 * XS, XS))
            ng[at] = ng[at] + nr[at]
            xs.start("far_p", j)
            xs.start("far_m", j)

    def sibs_here():
        for i in range(1, 4):
            sib.arrived("s", i)

    def ng_r(j):
        low, high = (trows(j), span(xp * XS, WS)), (trows(j), span(xp * XS + WS, WS))
        xs.arrived("far_p", j)
        ng[low] = ng[low] + nr[low] + xf[0, trows(j)]
        ng[high] = ng[high] + nr[high]
        xs.start("near_p", j)
        low, high = (trows(j), span(xm * XS, WS)), (trows(j), span(xm * XS + WS, WS))
        xs.arrived("far_m", j)
        ng[high] = ng[high] + nr[high] + xf[1, trows(j)]
        ng[low] = ng[low] + nr[low]
        xs.start("near_m", j)

    def ng_u(j):
        xs.arrived("near_p", j)
        xs.arrived("near_m", j)
        theirs, ours = span((1 - yh) * WS, WS), span(yh * WS, WS)
        base = x * XS
        for half, at in ((theirs, base + (1 - yh) * WS), (ours, base + yh * WS)):
            total = plus(
                ng[trows(j), span(at, WS)],
                nr[trows(j), span(at, WS)],
                xn[0, trows(j), half],
                xn[1, trows(j), half],
            )
            if half is theirs:
                hs[trows(j)] = total.astype(BF16)
                xs.start("h", j)
            else:
                ho[trows(j)] = total

    def ig_copy(j):
        return pltpu.make_async_copy(igv.at[trows(j)], ig_out.at[trows(j)], ig_sem.at[j])

    def ng_v(j):
        xs.arrived("h", j)
        scaled = plus(ho[trows(j)], hr[trows(j)]) * gain[:, span(wi * WS, WS)]
        scale = inv[trows(j)][:, :1]
        dots = rdacc[trows(j)][:, :1]
        igv[trows(j)] = (scale * scaled - tsl[trows(j)].astype(F32) * (scale * scale) * dots).astype(
            BF16
        )
        ig_copy(j).start()

    rds = Lane(rd_s, rd_r)
    rds.add("s", lambda k: rdo.at[1], lambda k: rdr, dev_c, lambda k: rdr, rdr)
    rws = Lane(rw_s, rw_r)
    for r in range(7):
        rws.add(str(r), lambda k: rdo.at[0], lambda k, r=r: rdw.at[r], dev_w[r],
                lambda k, r=r: rdw.at[r], rdr)

    def rd_1():
        ones = jnp.ones((8, BLK), F32)
        for half in range(2):
            rdo[half] = lax.dot_general(
                ones,
                rdacc[half * TOK : (half + 1) * TOK],
                (((1,), (1,)), ((), ())),
                precision=lax.Precision.HIGHEST,
                preferred_element_type=F32,
            )
        rds.start("s", 0)

    def rd_2():
        rds.arrived("s", 0)
        rdo[0] = rdo[0] + rdr[...]
        for r in range(7):
            rws.start(str(r), 0)

    def rd_3():
        load_tsl.wait()
        for r in range(7):
            rws.arrived(str(r), 0)
        total = rdo[0]
        for r in range(7):
            total = total + rdw[r]
        rdacc[pl.ds(0, TOK)] = jnp.broadcast_to((total / D).T[:, :1], (TOK, BLK))

    rotation = hadamard()

    def decoded(core, k):
        at = wide_cols(core, k)
        turned = jnp.dot(cod[:, at], rotation, preferred_element_type=F32)
        block = core * CH + k
        norm = 1.0 / (BLK**0.5)
        top = turned[:BLK] * (grid[codes[0, block]] * norm)
        low = turned[BLK:] * (grid[codes[1, block]] * norm)
        return jnp.concatenate([top, low], axis=0).astype(BF16)

    def decode(k):
        wsib[:, cols(k)] = decoded(1 - c, k)
        swap.start("w", k)
        w[yl, z, mine, cols(k)] = decoded(c, k)

    @pl.loop(0, CH)
    def _(k):
        decode(k)
        for i in range(LA):
            @pl.when(k == 2 * i + 2)
            def _(i=i):
                ag_a(i)

    cts.start("c", 0)

    def norm_tokens():
        rdacc[...] = jnp.zeros_like(rdacc)
        load_tok.wait()

        @pl.loop(0, NB)
        def _(j):
            @pl.loop(0, TB // 32)
            def _(i):
                rows = pl.ds(pl.multiple_of(j * TB + i * 32, 32), 32)
                values = ng[rows].astype(F32)
                scale = lax.rsqrt(
                    jnp.sum(values * values, axis=-1, keepdims=True) * (1.0 / D) + 1e-5
                )
                inv[rows] = jnp.broadcast_to(scale, (32, BLK))
                normed[rows] = (values * scale * gain[...]).astype(BF16)

            nms.start("n", j)

        load_cot.wait()

    def inputs_here():
        cts.arrived("c", 0)
        @pl.loop(0, NB)
        def _(j):
            nms.arrived("n", j)

    def at_step(s, fn, first, count, each=1):
        @pl.when((s >= first) & (s < first + count // each))
        def _():
            if each == 1:
                fn(s - first)
            else:

                @pl.loop(0, each)
                def _(i):
                    fn((s - first) * each + i)

    def once(s, fn, step):
        @pl.when(s == step)
        def _():
            fn()

    def several(fn, k, count):
        @pl.loop(0, count)
        def _(i):
            fn(k + i)

    done = CH - 1 + LD

    @pl.loop(0, STEPS)
    def _(s):
        at_step(s, lambda k: ag_a(k + LA), 0, CH - LA)
        at_step(s, ag_b, 0, CH)
        at_step(s, ag_c, LC, CH)
        once(s, norm_tokens, 0)
        once(s, inputs_here, LD)
        once(s, lambda: several(rs_a, 0, 4), CH)
        once(s, lambda: several(weight_part, 4, 3), done + 1)
        once(s, lambda: several(rs_a, 4, 3), done + 1)
        at_step(s, lambda k: rs_b(k + 2), done + 1, CH - 2)
        once(s, sibs_here, done + NR)
        at_step(s, ng_r, done + NR, NB, ER)
        at_step(s, rs_c, done + RC, CH)
        at_step(s, ng_u, done + NU, NB, EU)
        once(s, rd_1, done + 2)
        once(s, rd_2, done + 3)
        once(s, rd_3, done + 4)
        at_step(s, ng_v, done + NV, NB, EU)
        at_step(s, rs_d, done + RD, CH)
        once(s, lambda: several(weight_part, 0, 2), LD + 2)
        once(s, lambda: several(weight_part, 2, 2), LD + 4)
        at_step(s, ng_first, LD + 4, 4, 2)
        at_step(s, ag_d, LD, CH)

        @pl.when((s > LD) & (s < done) & ((s - LD) % 2 == 1))
        def _():
            forward(s - LD - 1, 2)

        once(s, lambda: forward(CH - 1, 1), done)

        @pl.when(s == done)
        def _():
            @pl.loop(0, 2)
            def _(i):
                rs_b(i)
                several(ng_p, 2 * i, 2)

            ng_q()

    for lane in (swap, ag, rs, nms, xs, sib, cts, rds, rws):
        lane.drain()

    @pl.loop(0, CH)
    def _(k):
        act_local(k).wait()
        act_remote(k).wait_send()
        act_remote(k, True).wait_recv()
        wg_local(k).wait()
        wg_remote(k).wait_send()
        wg_remote(k, True).wait_recv()

    @pl.loop(0, NB)
    def _(j):
        ig_copy(j).wait()


def per_device(tokens, norm_gain, coded, block_codes, grid, cotangent):
    anywhere = pl.BlockSpec(memory_space=pl.ANY)
    vmem = pl.BlockSpec(memory_space=pltpu.VMEM)
    smem = pl.BlockSpec(memory_space=pltpu.SMEM)
    sem = pltpu.SemaphoreType.DMA
    return pl.pallas_call(
        kernel,
        out_shape=(
            jax.ShapeDtypeStruct((TOK, CW), BF16),
            jax.ShapeDtypeStruct((D // 16, CW), F32),
            jax.ShapeDtypeStruct((TOK, WS), BF16),
        ),
        in_specs=[anywhere, vmem, anywhere, smem, smem, anywhere],
        out_specs=(anywhere, anywhere, anywhere),
        scratch_shapes=[
            pltpu.VMEM((256, CW), BF16),
            pltpu.VMEM((256, HALF), BF16),
            pltpu.VMEM((2, 4, CR, HALF), BF16),
            pltpu.VMEM((2 * TOK, D), BF16),
            pltpu.VMEM((2 * TOK, HALF), BF16),
            pltpu.VMEM((2 * TOK, HALF), BF16),
            pltpu.VMEM((2, 4, CR, HALF), BF16),
            pltpu.VMEM((CR, HALF), F32),
            pltpu.VMEM((2 * TOK, D), BF16),
            pltpu.VMEM((TOK, D), BF16),
            pltpu.VMEM((2, TOK, WS), BF16),
            pltpu.VMEM((2, TOK, XS), BF16),
            pltpu.VMEM((TOK, WS), BF16),
            pltpu.VMEM((TOK, WS), BF16),
            pltpu.VMEM((TOK, WS), F32),
            pltpu.VMEM((TOK, WS), BF16),
            pltpu.VMEM((TOK, WS), BF16),
            pltpu.VMEM((TOK, BLK), F32),
            pltpu.VMEM((2 * TOK, BLK), F32),
            pltpu.VMEM((2, 8, TOK), F32),
            pltpu.VMEM((8, TOK), F32),
            pltpu.VMEM((7, 8, TOK), F32),
            pltpu.VMEM((CH, 4, R1, BLK), BF16),
            pltpu.VMEM((2, CH, 2, H2, BLK), BF16),
            pltpu.VMEM((2, CH, H1, BLK), BF16),
            pltpu.VMEM((2, CH, 2, R2, BLK), BF16),
            pltpu.VMEM((2, CH, R1, BLK), BF16),
            pltpu.VMEM((CH, R2, BLK), BF16),
            sem((4,)), sem((3, CH)), sem((3, CH)), sem((NB,)),
            sem((12,)), sem((12, CH)), sem((10,)), sem((10, CH)), sem((1,)), sem((1, 4)),
            sem((1,)), sem((1, CH)), sem((1,)), sem((1, NB)), sem((5,)), sem((5, NB)),
            sem((1,)), sem((1, 1)), sem((7,)), sem((7, 1)), sem((1,)), sem((1, 1)),
        ],
        compiler_params=pltpu.CompilerParams(
            collective_id=0, has_side_effects=True, vmem_limit_bytes=63 << 20
        ),
        cost_estimate=pl.CostEstimate(
            flops=6 * TOK * D * CW, bytes_accessed=40 << 20, transcendentals=TOK * CW
        ),
    )(tokens, norm_gain.reshape(1, D), coded, block_codes, grid, cotangent)


def solution(mesh):
    placed = (
        P("narrow", None), P(), P("narrow", "wide"), P("narrow", "wide"), P(), P("narrow", "wide"),
    )
    return jax.shard_map(
        per_device,
        mesh=mesh,
        in_specs=placed,
        out_specs=(P("narrow", "wide"), P("narrow", "wide"), P("narrow", "wide")),
        check_vma=False,
    )
```

```python
import jax
import jax.numpy as jnp
from jax import lax
from jax.experimental import pallas as pl
from jax.experimental.pallas import tpu as pltpu
from jax.sharding import PartitionSpec as P

MESH = pl.DeviceIdType.MESH
F32, BF16 = jnp.float32, jnp.bfloat16

D = 4096
TOK = 512
CW = 1792
HALF = 896
BLK = 128
CH = HALF // BLK
CR = 512
G1 = 224
G2, GH = CR - G1, (CR - G1) // 2
R1 = 160
R2 = CR - R1
H1, H2 = R1 // 2, R2 // 2
KP = 4 * BLK
NB = 8
TB = TOK // NB
XS = D // 4
WS = D // 8

LA, LC, LD = 1, 1, 2
RC, RD = 1, 3
RE = 1
NR, NU, NV = 2, 3, 5
ER, EU = 2, 2
PARTS = 2
STEPS = CH - 1 + LD + max(CH + RD, NV + NB // EU)


def hadamard():
    both = lax.broadcasted_iota(jnp.int32, (BLK, BLK), 0) & lax.broadcasted_iota(
        jnp.int32, (BLK, BLK), 1
    )
    for shift in (4, 2, 1):
        both = both ^ lax.shift_right_logical(both, shift)
    return (1 - 2 * (both & 1)).astype(F32).astype(BF16)


class Lane:
    def __init__(self, send_sems, recv_sems):
        self.send_sems, self.recv_sems, self.kinds, self.rows = send_sems, recv_sems, {}, {}

    def add(self, name, src, dst, device, land, whole):
        self.rows[name] = len(self.kinds)
        self.kinds[name] = (src, dst, device, land, whole)

    def copy(self, name, k, src, dst):
        row = self.rows[name]
        return pltpu.make_async_remote_copy(
            src_ref=src,
            dst_ref=dst,
            send_sem=self.send_sems.at[row],
            recv_sem=self.recv_sems.at[row, k],
            device_id=self.kinds[name][2],
            device_id_type=MESH,
        )

    def start(self, name, k):
        src, dst, _, _, _ = self.kinds[name]
        self.copy(name, k, src(k), dst(k)).start()

    def arrived(self, name, k):
        land = self.kinds[name][3]
        self.copy(name, k, land(k), land(k)).wait_recv()

    def drain(self):
        for name, (_, _, _, _, whole) in self.kinds.items():
            self.copy(name, 0, whole, whole).wait_send()


def kernel(
    tokens, gain, coded, codes, grid, cot,
    act_out, wg_out, ig_out,
    cod, wsib, w, normed, pg, act, g, fin,
    ng, nr, xf, xn, hs, hr, ho, tsl, igv,
    inv, rdacc, rdo, rdr, rdw,
    ry1, rf, rg, rn, rm, ry2,
    loc, act_sem, wg_sem, ig_sem,
    ag_s, ag_r, rs_s, rs_r, si_s, si_r, sw_s, sw_r, nm_s, nm_r, x_s, x_r, rd_s, rd_r, rw_s, rw_r, ct_s, ct_r,
):
    wi, ni = lax.axis_index("wide"), lax.axis_index("narrow")
    x, yh = wi // 2, wi % 2
    yl, z, c = ni // 8, (ni // 2) % 4, ni % 2
    zp, zm, z2 = (z + 1) % 4, (z + 3) % 4, (z + 2) % 4
    xp, xm, x2 = (x + 1) % 4, (x + 3) % 4, (x + 2) % 4
    yo = 1 - yl
    dev_zp = (wi, (yl * 4 + zp) * 2 + c)
    dev_zm = (wi, (yl * 4 + zm) * 2 + c)
    dev_y = (wi, (yo * 4 + z) * 2 + c)
    dev_c = (wi, (yl * 4 + z) * 2 + (1 - c))
    dev_xp = (xp * 2 + yh, ni)
    dev_xm = (xm * 2 + yh, ni)
    dev_h = (x * 2 + (1 - yh), ni)
    dev_w = [((wi + r) % 8, ni) for r in range(1, 8)]

    def cols(k):
        return pl.ds(pl.multiple_of(k * BLK, BLK), BLK)

    def wide_cols(core, k):
        return pl.ds(pl.multiple_of(core * HALF + k * BLK, BLK), BLK)

    def trows(j, base=0):
        return pl.ds(pl.multiple_of(base + j * TB, TB), TB)

    mine = pl.ds(pl.multiple_of(c * 256, 256), 256)
    other = pl.ds(pl.multiple_of((1 - c) * 256, 256), 256)

    load_cod = pltpu.make_async_copy(coded, cod, loc.at[0])
    load_tok = pltpu.make_async_copy(tokens, ng.at[pl.ds(0, TOK)], loc.at[1])
    load_cot = pltpu.make_async_copy(
        cot.at[:, pl.ds(pl.multiple_of(c * HALF, BLK), HALF)], pg.at[pl.ds(0, TOK)], loc.at[2]
    )
    load_tsl = pltpu.make_async_copy(
        tokens.at[:, pl.ds(pl.multiple_of(wi * WS, BLK), WS)], tsl, loc.at[3]
    )
    load_cod.start()
    barrier = pltpu.get_barrier_semaphore()
    partners = [dev_zp, dev_zm, dev_y, dev_c, *dev_w]
    for device in partners:
        pl.semaphore_signal(barrier, inc=1, device_id=device, device_id_type=MESH)
    load_tok.start()
    load_cot.start()
    load_tsl.start()
    load_cod.wait()
    pl.semaphore_wait(barrier, len(partners))

    swap = Lane(sw_s, sw_r)
    swap.add(
        "w",
        lambda k: wsib.at[:, cols(k)],
        lambda k: w.at[yl, z, mine, cols(k)],
        dev_c,
        lambda k: w.at[yl, z, other, cols(k)],
        wsib,
    )
    cts = Lane(ct_s, ct_r)
    cts.add(
        "c",
        lambda k: cot.at[:, pl.ds(pl.multiple_of((1 - c) * HALF, BLK), HALF)],
        lambda k: pg.at[pl.ds(TOK, TOK)],
        dev_c,
        lambda k: pg.at[pl.ds(TOK, TOK)],
        pg.at[pl.ds(TOK, TOK)],
    )
    nms = Lane(nm_s, nm_r)
    nms.add(
        "n",
        lambda j: normed.at[trows(j)],
        lambda j: normed.at[trows(j, TOK)],
        dev_c,
        lambda j: normed.at[trows(j, TOK)],
        normed.at[pl.ds(TOK, TOK)],
    )

    ag = Lane(ag_s, ag_r)

    def piece(name, device, src_at, land_at, lo, n):
        piece_of(name, device, src_at, land_at, pl.ds(lo, n))

    def piece_of(name, device, src_at, land_at, rows):
        ag.add(
            name,
            lambda k: w.at[src_at[0], src_at[1], rows, cols(k)],
            lambda k: w.at[src_at[0], src_at[1], rows, cols(k)],
            device,
            lambda k: w.at[land_at[0], land_at[1], rows, cols(k)],
            w.at[src_at[0], src_at[1], rows],
        )

    for half, rows in (("mine", mine), ("other", other)):
        piece_of("zp_" + half, dev_zp, (yl, z), (yl, zm), rows)
        piece_of("zm_" + half, dev_zm, (yl, z), (yl, zp), rows)
        piece_of("y_" + half, dev_y, (yl, z), (yo, z), rows)
    piece("far_zp", dev_zp, (yl, zm), (yl, z2), 0, CR // 2)
    piece("far_zm", dev_zm, (yl, zp), (yl, z2), CR // 2, CR // 2)
    piece("zm_y", dev_y, (yl, zm), (yo, zm), 0, G1)
    piece("zp_y", dev_y, (yl, zp), (yo, zp), 0, G1)
    piece("y_zp", dev_zp, (yo, z), (yo, zm), G1, G2)
    piece("y_zm", dev_zm, (yo, z), (yo, zp), G1, G2)
    piece("z2_y", dev_y, (yl, z2), (yo, z2), 0, G1)
    piece("yfar_zp", dev_zp, (yo, zm), (yo, z2), G1, GH)
    piece("yfar_zm", dev_zm, (yo, zp), (yo, z2), G1 + GH, GH)

    def ag_own(k, half):
        ag.start("zp_" + half, k)
        ag.start("zm_" + half, k)
        ag.start("y_" + half, k)

    def ag_a(k):
        ag_own(k, "mine")
        swap.arrived("w", k)
        ag_own(k, "other")

    def ag_b(k):
        ag.arrived("y_mine", k)
        ag.arrived("y_other", k)
        ag.start("y_zp", k)
        ag.start("y_zm", k)
        ag.arrived("zp_mine", k)
        ag.arrived("zp_other", k)
        ag.start("far_zp", k)
        ag.start("zm_y", k)
        ag.arrived("zm_mine", k)
        ag.arrived("zm_other", k)
        ag.start("far_zm", k)
        ag.start("zp_y", k)

    def ag_c(k):
        ag.arrived("far_zp", k)
        ag.start("z2_y", k)
        ag.arrived("y_zp", k)
        ag.start("yfar_zp", k)
        ag.arrived("y_zm", k)
        ag.start("yfar_zm", k)

    def ag_d(k):
        for name in ("far_zm", "zm_y", "zp_y", "z2_y", "yfar_zp", "yfar_zm"):
            ag.arrived(name, k)

    rs = Lane(rs_s, rs_r)
    rs.add("a_y", lambda k: g.at[yo, :, pl.ds(0, R1), cols(k)], lambda k: ry1.at[k], dev_y,
           lambda k: ry1.at[k], g.at[yo, :, pl.ds(0, R1)])
    rs.add("a_zp", lambda k: g.at[:, z2, pl.ds(R1, H2), cols(k)], lambda k: rf.at[0, k], dev_zp,
           lambda k: rf.at[0, k], g.at[:, z2, pl.ds(R1, H2)])
    rs.add("a_zm", lambda k: g.at[:, z2, pl.ds(R1 + H2, H2), cols(k)], lambda k: rf.at[1, k],
           dev_zm, lambda k: rf.at[1, k], g.at[:, z2, pl.ds(R1 + H2, H2)])
    rs.add("b1_zp", lambda k: g.at[yl, z2, pl.ds(0, H1), cols(k)], lambda k: rg.at[0, k], dev_zp,
           lambda k: rg.at[0, k], g.at[yl, z2, pl.ds(0, H1)])
    rs.add("b1_zm", lambda k: g.at[yl, z2, pl.ds(H1, H1), cols(k)], lambda k: rg.at[1, k], dev_zm,
           lambda k: rg.at[1, k], g.at[yl, z2, pl.ds(H1, H1)])
    rs.add("b2_zp", lambda k: g.at[:, zp, pl.ds(R1, R2), cols(k)], lambda k: rn.at[0, k], dev_zp,
           lambda k: rn.at[0, k], g.at[:, zp, pl.ds(R1, R2)])
    rs.add("b2_zm", lambda k: g.at[:, zm, pl.ds(R1, R2), cols(k)], lambda k: rn.at[1, k], dev_zm,
           lambda k: rn.at[1, k], g.at[:, zm, pl.ds(R1, R2)])
    rs.add("c_zp", lambda k: g.at[yl, zp, pl.ds(0, R1), cols(k)], lambda k: rm.at[0, k], dev_zp,
           lambda k: rm.at[0, k], g.at[yl, zp, pl.ds(0, R1)])
    rs.add("c_zm", lambda k: g.at[yl, zm, pl.ds(0, R1), cols(k)], lambda k: rm.at[1, k], dev_zm,
           lambda k: rm.at[1, k], g.at[yl, zm, pl.ds(0, R1)])
    rs.add("c_y", lambda k: g.at[yo, z, pl.ds(R1, R2), cols(k)], lambda k: ry2.at[k], dev_y,
           lambda k: ry2.at[k], g.at[yo, z, pl.ds(R1, R2)])

    def plus(first, *rest):
        total = first.astype(F32)
        for term in rest:
            total = total + term.astype(F32)
        return total

    def add_into(at, *terms):
        total = g[at]
        for term in terms:
            total = total + term
        g[at] = total

    def rs_a(k):
        rs.start("a_y", k)
        rs.start("a_zp", k)
        rs.start("a_zm", k)

    def rs_b(k):
        rs.arrived("a_zp", k)
        add_into((slice(None), zp, pl.ds(R1, H2), cols(k)), rf[0, k])
        rs.start("b2_zp", k)
        rs.arrived("a_zm", k)
        add_into((slice(None), zm, pl.ds(R1 + H2, H2), cols(k)), rf[1, k])
        rs.start("b2_zm", k)
        rs.arrived("a_y", k)
        add_into((yl, slice(None), pl.ds(0, R1), cols(k)), ry1[k])
        rs.start("b1_zp", k)
        rs.start("b1_zm", k)

    def rs_c(k):
        rs.arrived("b2_zp", k)
        rs.arrived("b2_zm", k)
        add_into((slice(None), z, pl.ds(R1, R2), cols(k)), rn[0, k], rn[1, k])
        rs.start("c_y", k)
        rs.arrived("b1_zp", k)
        add_into((yl, zp, pl.ds(0, H1), cols(k)), rg[0, k])
        rs.start("c_zp", k)
        rs.arrived("b1_zm", k)
        add_into((yl, zm, pl.ds(H1, H1), cols(k)), rg[1, k])
        rs.start("c_zm", k)

    def wg_local(k):
        return pltpu.make_async_copy(
            fin.at[mine, cols(k)], wg_out.at[:, wide_cols(c, k)], wg_sem.at[0, k]
        )

    def wg_remote(k, landed=False):
        target = wg_out.at[:, wide_cols((1 - c) if landed else c, k)]
        return pltpu.make_async_remote_copy(
            src_ref=fin.at[other, cols(k)],
            dst_ref=target,
            send_sem=wg_sem.at[1, k],
            recv_sem=wg_sem.at[2, k],
            device_id=dev_c,
            device_id_type=MESH,
        )

    def rs_d(k):
        rs.arrived("c_zp", k)
        rs.arrived("c_zm", k)
        fin[pl.ds(0, R1), cols(k)] = plus(g[yl, z, pl.ds(0, R1), cols(k)], rm[0, k], rm[1, k])
        rs.arrived("c_y", k)
        fin[pl.ds(R1, R2), cols(k)] = plus(g[yl, z, pl.ds(R1, R2), cols(k)], ry2[k])
        wg_local(k).start()
        wg_remote(k).start()

    def act_local(k):
        return pltpu.make_async_copy(
            act.at[pl.ds(0, TOK), cols(k)], act_out.at[:, wide_cols(c, k)], act_sem.at[0, k]
        )

    def act_remote(k, landed=False):
        return pltpu.make_async_remote_copy(
            src_ref=act.at[pl.ds(TOK, TOK), cols(k)],
            dst_ref=act_out.at[:, wide_cols((1 - c) if landed else c, k)],
            send_sem=act_sem.at[1, k],
            recv_sem=act_sem.at[2, k],
            device_id=dev_c,
            device_id_type=MESH,
        )

    def forward(k, count):
        at = pl.ds(pl.multiple_of(k * BLK, BLK), count * BLK)

        @pl.loop(0, 4)
        def _(t):
            rows = pl.ds(pl.multiple_of(t * 256, 256), 256)
            weight = w[:, :, :, at].reshape(D, count * BLK)
            preact = jnp.dot(normed[rows], weight, preferred_element_type=F32)
            sig = 1.0 / (1.0 + jnp.exp(-preact))
            act[rows, at] = (preact * sig).astype(BF16)
            grad = (pg[rows, at].astype(F32) * sig * (1.0 + preact * (1.0 - sig))).astype(BF16)
            pg[rows, at] = grad
            dots = preact * grad.astype(F32)
            for i in range(count):
                rdacc[rows] += dots[:, i * BLK : (i + 1) * BLK]

        for i in range(count):
            act_local(k + i).start()
            act_remote(k + i).start()

    def weight_part(k):
        turned = pg[:, cols(k)].T
        for q in range(8):
            part = jnp.dot(turned, normed[:, q * CR : (q + 1) * CR], preferred_element_type=F32)
            g[q // 4, q % 4, :, cols(k)] = part.T.astype(BF16)

    xs = Lane(x_s, x_r)

    def span(start, n):
        return pl.ds(pl.multiple_of(start, BLK), n)

    xs.add("far_p", lambda j: ng.at[trows(j), span(x2 * XS, WS)], lambda j: xf.at[0, trows(j)],
           dev_xp, lambda j: xf.at[0, trows(j)], ng.at[pl.ds(0, TOK), span(0, WS)])
    xs.add("far_m", lambda j: ng.at[trows(j), span(x2 * XS + WS, WS)], lambda j: xf.at[1, trows(j)],
           dev_xm, lambda j: xf.at[1, trows(j)], ng.at[pl.ds(0, TOK), span(0, WS)])
    xs.add("near_p", lambda j: ng.at[trows(j), span(xp * XS, XS)], lambda j: xn.at[0, trows(j)],
           dev_xp, lambda j: xn.at[0, trows(j)], ng.at[pl.ds(0, TOK), span(0, XS)])
    xs.add("near_m", lambda j: ng.at[trows(j), span(xm * XS, XS)], lambda j: xn.at[1, trows(j)],
           dev_xm, lambda j: xn.at[1, trows(j)], ng.at[pl.ds(0, TOK), span(0, XS)])
    xs.add("h", lambda j: hs.at[trows(j)], lambda j: hr.at[trows(j)], dev_h,
           lambda j: hr.at[trows(j)], hs)

    def quarter(i):
        m, n = i // 2, i % 2
        return (x + 2 - n + m * (1 - 2 * n)) % 4

    sib = Lane(si_s, si_r)
    sib.add(
        "s",
        lambda i: ng.at[pl.ds(TOK, TOK), span(quarter(i) * XS, XS)],
        lambda i: nr.at[:, span(quarter(i) * XS, XS)],
        dev_c,
        lambda i: nr.at[:, span(quarter(i) * XS, XS)],
        nr,
    )

    def grads_times_weight(i, t, lo, n, first):
        rows = pl.ds(pl.multiple_of((1 - t) * TOK, TOK), TOK)
        for h in range(2):
            block = quarter(i) * 2 + h
            part = lax.dot_general(
                pg[rows, lo : lo + n],
                w[block // 4, block % 4, :, lo : lo + n],
                (((1,), (1,)), ((), ())),
                preferred_element_type=F32,
            )
            at = (rows, span(block * CR, CR))
            ng[at] = part.astype(BF16) if first else plus(part, ng[at]).astype(BF16)

    def ng_first(i):
        @pl.loop(0, 2)
        def _(t):
            grads_times_weight(i, t, 0, KP, True)

    def ng_p(i):
        @pl.loop(0, 2)
        def _(t):
            grads_times_weight(i, t, KP, HALF - KP, False)

            @pl.when(t == 0)
            def _():
                sib.start("s", i)

    def ng_q():
        sib.arrived("s", 0)

        @pl.loop(0, NB)
        def _(j):
            at = (trows(j), span(x2 * XS, XS))
            ng[at] = ng[at] + nr[at]
            xs.start("far_p", j)
            xs.start("far_m", j)

    def sibs_here():
        for i in range(1, 4):
            sib.arrived("s", i)

    def ng_r(j):
        low, high = (trows(j), span(xp * XS, WS)), (trows(j), span(xp * XS + WS, WS))
        xs.arrived("far_p", j)
        ng[low] = ng[low] + nr[low] + xf[0, trows(j)]
        ng[high] = ng[high] + nr[high]
        xs.start("near_p", j)
        low, high = (trows(j), span(xm * XS, WS)), (trows(j), span(xm * XS + WS, WS))
        xs.arrived("far_m", j)
        ng[high] = ng[high] + nr[high] + xf[1, trows(j)]
        ng[low] = ng[low] + nr[low]
        xs.start("near_m", j)

    def ng_u(j):
        xs.arrived("near_p", j)
        xs.arrived("near_m", j)
        theirs, ours = span((1 - yh) * WS, WS), span(yh * WS, WS)
        base = x * XS
        for half, at in ((theirs, base + (1 - yh) * WS), (ours, base + yh * WS)):
            total = plus(
                ng[trows(j), span(at, WS)],
                nr[trows(j), span(at, WS)],
                xn[0, trows(j), half],
                xn[1, trows(j), half],
            )
            if half is theirs:
                hs[trows(j)] = total.astype(BF16)
                xs.start("h", j)
            else:
                ho[trows(j)] = total

    def ig_copy(j):
        return pltpu.make_async_copy(igv.at[trows(j)], ig_out.at[trows(j)], ig_sem.at[j])

    def ng_v(j):
        xs.arrived("h", j)
        scaled = plus(ho[trows(j)], hr[trows(j)]) * gain[:, span(wi * WS, WS)]
        scale = inv[trows(j)][:, :1]
        dots = rdacc[trows(j)][:, :1]
        igv[trows(j)] = (scale * scaled - tsl[trows(j)].astype(F32) * (scale * scale) * dots).astype(
            BF16
        )
        ig_copy(j).start()

    rds = Lane(rd_s, rd_r)
    rds.add("s", lambda k: rdo.at[1], lambda k: rdr, dev_c, lambda k: rdr, rdr)
    rws = Lane(rw_s, rw_r)
    for r in range(7):
        rws.add(str(r), lambda k: rdo.at[0], lambda k, r=r: rdw.at[r], dev_w[r],
                lambda k, r=r: rdw.at[r], rdr)

    def rd_1():
        ones = jnp.ones((8, BLK), F32)
        for half in range(2):
            rdo[half] = lax.dot_general(
                ones,
                rdacc[half * TOK : (half + 1) * TOK],
                (((1,), (1,)), ((), ())),
                precision=lax.Precision.HIGHEST,
                preferred_element_type=F32,
            )
        rds.start("s", 0)

    def rd_2():
        rds.arrived("s", 0)
        rdo[0] = rdo[0] + rdr[...]
        for r in range(7):
            rws.start(str(r), 0)

    def rd_3():
        load_tsl.wait()
        for r in range(7):
            rws.arrived(str(r), 0)
        total = rdo[0]
        for r in range(7):
            total = total + rdw[r]
        rdacc[pl.ds(0, TOK)] = jnp.broadcast_to((total / D).T[:, :1], (TOK, BLK))

    rotation = hadamard()

    def decoded(core, k):
        at = wide_cols(core, k)
        turned = jnp.dot(cod[:, at], rotation, preferred_element_type=F32)
        block = core * CH + k
        norm = 1.0 / (BLK**0.5)
        top = turned[:BLK] * (grid[codes[0, block]] * norm)
        low = turned[BLK:] * (grid[codes[1, block]] * norm)
        return jnp.concatenate([top, low], axis=0).astype(BF16)

    def decode(k):
        wsib[:, cols(k)] = decoded(1 - c, k)
        swap.start("w", k)
        w[yl, z, mine, cols(k)] = decoded(c, k)

    decode(0)
    ag_own(0, "mine")

    @pl.loop(1, CH)
    def _(k):
        decode(k)

    swap.arrived("w", 0)
    ag_own(0, "other")
    for i in range(1, LA):
        ag_a(i)

    cts.start("c", 0)

    def norm_tokens():
        rdacc[...] = jnp.zeros_like(rdacc)
        load_tok.wait()

        @pl.loop(0, NB)
        def _(j):
            @pl.loop(0, TB // 32)
            def _(i):
                rows = pl.ds(pl.multiple_of(j * TB + i * 32, 32), 32)
                values = ng[rows].astype(F32)
                scale = lax.rsqrt(
                    jnp.sum(values * values, axis=-1, keepdims=True) * (1.0 / D) + 1e-5
                )
                inv[rows] = jnp.broadcast_to(scale, (32, BLK))
                normed[rows] = (values * scale * gain[...]).astype(BF16)

            nms.start("n", j)

        load_cot.wait()

    def inputs_here():
        cts.arrived("c", 0)
        @pl.loop(0, NB)
        def _(j):
            nms.arrived("n", j)

    def at_step(s, fn, first, count, each=1):
        @pl.when((s >= first) & (s < first + count // each))
        def _():
            if each == 1:
                fn(s - first)
            else:

                @pl.loop(0, each)
                def _(i):
                    fn((s - first) * each + i)

    def once(s, fn, step):
        @pl.when(s == step)
        def _():
            fn()

    def several(fn, k, count):
        @pl.loop(0, count)
        def _(i):
            fn(k + i)

    done = CH - 1 + LD

    @pl.loop(0, STEPS)
    def _(s):
        at_step(s, lambda k: ag_a(k + LA), 0, CH - LA)
        at_step(s, ag_b, 0, CH)
        at_step(s, ag_c, LC, CH)
        once(s, norm_tokens, 0)
        once(s, inputs_here, LD)
        once(s, lambda: several(rs_a, 0, RE), CH - 1)
        once(s, lambda: several(rs_a, RE, 4 - RE), CH)
        once(s, lambda: several(weight_part, 4, 3), done + 1)
        once(s, lambda: several(rs_a, 4, 3), done + 1)
        at_step(s, lambda k: rs_b(k + 2), done + 1, CH - 2)
        once(s, sibs_here, done + NR)
        at_step(s, ng_r, done + NR, NB, ER)
        at_step(s, rs_c, done + RC, CH)
        at_step(s, ng_u, done + NU, NB, EU)
        once(s, rd_1, done + 2)
        once(s, rd_2, done + 3)
        once(s, rd_3, done + 4)
        at_step(s, ng_v, done + NV, NB, EU)
        at_step(s, rs_d, done + RD, CH)
        once(s, lambda: several(weight_part, 0, 2), LD + 2)
        once(s, lambda: several(weight_part, 2, 2), LD + 4)
        at_step(s, ng_first, LD + 4, 4, 2)
        at_step(s, ag_d, LD, CH)

        @pl.when((s > LD) & (s < done) & ((s - LD) % 2 == 1))
        def _():
            forward(s - LD - 1, 2)

        once(s, lambda: forward(CH - 1, 1), done)

        @pl.when(s == done)
        def _():
            @pl.loop(0, 2)
            def _(i):
                rs_b(i)
                several(ng_p, 2 * i, 2)

            ng_q()

    for lane in (swap, ag, rs, nms, xs, sib, cts, rds, rws):
        lane.drain()

    @pl.loop(0, CH)
    def _(k):
        act_local(k).wait()
        act_remote(k).wait_send()
        act_remote(k, True).wait_recv()
        wg_local(k).wait()
        wg_remote(k).wait_send()
        wg_remote(k, True).wait_recv()

    @pl.loop(0, NB)
    def _(j):
        ig_copy(j).wait()


def hand_over(act, wg, ig, act_out, wg_out, ig_out, act_v, wg_v, ig_v, sems):
    loads, stores = [], []
    for i, (src, mid, dst) in enumerate(
        ((act, act_v, act_out), (wg, wg_v, wg_out), (ig, ig_v, ig_out))
    ):
        rows = src.shape[0] // PARTS
        for part in range(PARTS):
            at = pl.ds(part * rows, rows)
            loads.append(pltpu.make_async_copy(src.at[at], mid.at[at], sems.at[0, i, part]))
            stores.append(pltpu.make_async_copy(mid.at[at], dst.at[at], sems.at[1, i, part]))
    for load in loads:
        load.start()
    for load, store in zip(loads, stores):
        load.wait()
        store.start()
    for store in stores:
        store.wait()


def per_device(tokens, norm_gain, coded, block_codes, grid, cotangent):
    anywhere = pl.BlockSpec(memory_space=pl.ANY)
    vmem = pl.BlockSpec(memory_space=pltpu.VMEM)
    smem = pl.BlockSpec(memory_space=pltpu.SMEM)
    sem = pltpu.SemaphoreType.DMA
    results = pl.pallas_call(
        kernel,
        out_shape=(
            jax.ShapeDtypeStruct((TOK, CW), BF16),
            jax.ShapeDtypeStruct((D // 16, CW), F32),
            jax.ShapeDtypeStruct((TOK, WS), BF16),
        ),
        in_specs=[anywhere, vmem, anywhere, smem, smem, anywhere],
        out_specs=(anywhere, anywhere, anywhere),
        scratch_shapes=[
            pltpu.VMEM((256, CW), BF16),
            pltpu.VMEM((256, HALF), BF16),
            pltpu.VMEM((2, 4, CR, HALF), BF16),
            pltpu.VMEM((2 * TOK, D), BF16),
            pltpu.VMEM((2 * TOK, HALF), BF16),
            pltpu.VMEM((2 * TOK, HALF), BF16),
            pltpu.VMEM((2, 4, CR, HALF), BF16),
            pltpu.VMEM((CR, HALF), F32),
            pltpu.VMEM((2 * TOK, D), BF16),
            pltpu.VMEM((TOK, D), BF16),
            pltpu.VMEM((2, TOK, WS), BF16),
            pltpu.VMEM((2, TOK, XS), BF16),
            pltpu.VMEM((TOK, WS), BF16),
            pltpu.VMEM((TOK, WS), BF16),
            pltpu.VMEM((TOK, WS), F32),
            pltpu.VMEM((TOK, WS), BF16),
            pltpu.VMEM((TOK, WS), BF16),
            pltpu.VMEM((TOK, BLK), F32),
            pltpu.VMEM((2 * TOK, BLK), F32),
            pltpu.VMEM((2, 8, TOK), F32),
            pltpu.VMEM((8, TOK), F32),
            pltpu.VMEM((7, 8, TOK), F32),
            pltpu.VMEM((CH, 4, R1, BLK), BF16),
            pltpu.VMEM((2, CH, 2, H2, BLK), BF16),
            pltpu.VMEM((2, CH, H1, BLK), BF16),
            pltpu.VMEM((2, CH, 2, R2, BLK), BF16),
            pltpu.VMEM((2, CH, R1, BLK), BF16),
            pltpu.VMEM((CH, R2, BLK), BF16),
            sem((4,)), sem((3, CH)), sem((3, CH)), sem((NB,)),
            sem((15,)), sem((15, CH)), sem((10,)), sem((10, CH)), sem((1,)), sem((1, 4)),
            sem((1,)), sem((1, CH)), sem((1,)), sem((1, NB)), sem((5,)), sem((5, NB)),
            sem((1,)), sem((1, 1)), sem((7,)), sem((7, 1)), sem((1,)), sem((1, 1)),
        ],
        compiler_params=pltpu.CompilerParams(
            collective_id=0, has_side_effects=True, vmem_limit_bytes=63 << 20
        ),
        cost_estimate=pl.CostEstimate(
            flops=6 * TOK * D * CW, bytes_accessed=40 << 20, transcendentals=TOK * CW
        ),
    )(tokens, norm_gain.reshape(1, D), coded, block_codes, grid, cotangent)
    return pl.pallas_call(
        hand_over,
        out_shape=tuple(jax.ShapeDtypeStruct(r.shape, r.dtype) for r in results),
        in_specs=[anywhere] * 3,
        out_specs=(anywhere,) * 3,
        scratch_shapes=[pltpu.VMEM(r.shape, r.dtype) for r in results] + [sem((2, 3, PARTS))],
        compiler_params=pltpu.CompilerParams(vmem_limit_bytes=63 << 20),
    )(*results)


def solution(mesh):
    placed = (
        P("narrow", None), P(), P("narrow", "wide"), P("narrow", "wide"), P(), P("narrow", "wide"),
    )
    return jax.shard_map(
        per_device,
        mesh=mesh,
        in_specs=placed,
        out_specs=(P("narrow", "wide"), P("narrow", "wide"), P("narrow", "wide")),
        check_vma=False,
    )
```

```python
import jax
import jax.numpy as jnp
from jax import lax
from jax.experimental import pallas as pl
from jax.experimental.pallas import tpu as pltpu
from jax.sharding import PartitionSpec as P

MESH = pl.DeviceIdType.MESH
F32, BF16 = jnp.float32, jnp.bfloat16

D = 4096
TOK = 512
CW = 1792
HALF = 896
BLK = 128
CH = HALF // BLK
CR = 512
G1 = 224
G2, GH = CR - G1, (CR - G1) // 2
R1 = 160
R2 = CR - R1
H1, H2 = R1 // 2, R2 // 2
KP = 4 * BLK
NB = 8
TB = TOK // NB
XS = D // 4
WS = D // 8

LA, LC, LD = 1, 1, 2
RC, RD = 1, 3
RE = 1
NR, NU, NV = 2, 3, 5
ER, EU = 2, 2
PARTS = 2
STEPS = CH - 1 + LD + max(CH + RD, NV + NB // EU)


def hadamard():
    both = lax.broadcasted_iota(jnp.int32, (BLK, BLK), 0) & lax.broadcasted_iota(
        jnp.int32, (BLK, BLK), 1
    )
    for shift in (4, 2, 1):
        both = both ^ lax.shift_right_logical(both, shift)
    return (1 - 2 * (both & 1)).astype(F32).astype(BF16)


class Lane:
    def __init__(self, send_sems, recv_sems):
        self.send_sems, self.recv_sems, self.kinds, self.rows = send_sems, recv_sems, {}, {}

    def add(self, name, src, dst, device, land, whole):
        self.rows[name] = len(self.kinds)
        self.kinds[name] = (src, dst, device, land, whole)

    def copy(self, name, k, src, dst):
        row = self.rows[name]
        return pltpu.make_async_remote_copy(
            src_ref=src,
            dst_ref=dst,
            send_sem=self.send_sems.at[row],
            recv_sem=self.recv_sems.at[row, k],
            device_id=self.kinds[name][2],
            device_id_type=MESH,
        )

    def start(self, name, k):
        src, dst, _, _, _ = self.kinds[name]
        self.copy(name, k, src(k), dst(k)).start()

    def arrived(self, name, k):
        land = self.kinds[name][3]
        self.copy(name, k, land(k), land(k)).wait_recv()

    def drain(self):
        for name, (_, _, _, _, whole) in self.kinds.items():
            self.copy(name, 0, whole, whole).wait_send()


def kernel(
    tokens, gain, coded, codes, grid, cot,
    act_out, wg_out, ig_out,
    cod, wsib, w, normed, pg, act, g, fin,
    ng, nr, xf, xn, hs, hr, ho, tsl, igv,
    inv, rdacc, rdo, rdr, rdw,
    ry1, rf, rg, rn, rm, ry2,
    loc, act_sem, wg_sem, ig_sem,
    ag_s, ag_r, rs_s, rs_r, si_s, si_r, sw_s, sw_r, nm_s, nm_r, x_s, x_r, rd_s, rd_r, rw_s, rw_r, ct_s, ct_r,
):
    wi, ni = lax.axis_index("wide"), lax.axis_index("narrow")
    x, yh = wi // 2, wi % 2
    yl, z, c = ni // 8, (ni // 2) % 4, ni % 2
    zp, zm, z2 = (z + 1) % 4, (z + 3) % 4, (z + 2) % 4
    xp, xm, x2 = (x + 1) % 4, (x + 3) % 4, (x + 2) % 4
    yo = 1 - yl
    dev_zp = (wi, (yl * 4 + zp) * 2 + c)
    dev_zm = (wi, (yl * 4 + zm) * 2 + c)
    dev_y = (wi, (yo * 4 + z) * 2 + c)
    dev_c = (wi, (yl * 4 + z) * 2 + (1 - c))
    dev_xp = (xp * 2 + yh, ni)
    dev_xm = (xm * 2 + yh, ni)
    dev_h = (x * 2 + (1 - yh), ni)
    dev_w = [((wi + r) % 8, ni) for r in range(1, 8)]

    def cols(k):
        return pl.ds(pl.multiple_of(k * BLK, BLK), BLK)

    def wide_cols(core, k):
        return pl.ds(pl.multiple_of(core * HALF + k * BLK, BLK), BLK)

    def trows(j, base=0):
        return pl.ds(pl.multiple_of(base + j * TB, TB), TB)

    mine = pl.ds(pl.multiple_of(c * 256, 256), 256)
    other = pl.ds(pl.multiple_of((1 - c) * 256, 256), 256)

    load_cod = pltpu.make_async_copy(coded, cod, loc.at[0])
    load_tok = pltpu.make_async_copy(tokens, ng.at[pl.ds(0, TOK)], loc.at[1])
    load_cot = pltpu.make_async_copy(
        cot.at[:, pl.ds(pl.multiple_of(c * HALF, BLK), HALF)], pg.at[pl.ds(0, TOK)], loc.at[2]
    )
    load_tsl = pltpu.make_async_copy(
        tokens.at[:, pl.ds(pl.multiple_of(wi * WS, BLK), WS)], tsl, loc.at[3]
    )
    load_cod.start()
    barrier = pltpu.get_barrier_semaphore()
    partners = [dev_zp, dev_zm, dev_y, dev_c, *dev_w]
    for device in partners:
        pl.semaphore_signal(barrier, inc=1, device_id=device, device_id_type=MESH)
    load_tok.start()
    load_cot.start()
    load_tsl.start()
    load_cod.wait()
    pl.semaphore_wait(barrier, len(partners))

    swap = Lane(sw_s, sw_r)
    swap.add(
        "w",
        lambda k: wsib.at[:, cols(k)],
        lambda k: w.at[yl, z, mine, cols(k)],
        dev_c,
        lambda k: w.at[yl, z, other, cols(k)],
        wsib,
    )
    cts = Lane(ct_s, ct_r)
    cts.add(
        "c",
        lambda k: cot.at[:, pl.ds(pl.multiple_of((1 - c) * HALF, BLK), HALF)],
        lambda k: pg.at[pl.ds(TOK, TOK)],
        dev_c,
        lambda k: pg.at[pl.ds(TOK, TOK)],
        pg.at[pl.ds(TOK, TOK)],
    )
    nms = Lane(nm_s, nm_r)
    nms.add(
        "n",
        lambda j: normed.at[trows(j)],
        lambda j: normed.at[trows(j, TOK)],
        dev_c,
        lambda j: normed.at[trows(j, TOK)],
        normed.at[pl.ds(TOK, TOK)],
    )

    ag = Lane(ag_s, ag_r)

    def piece(name, device, src_at, land_at, lo, n):
        piece_of(name, device, src_at, land_at, pl.ds(lo, n))

    def piece_of(name, device, src_at, land_at, rows):
        ag.add(
            name,
            lambda k: w.at[src_at[0], src_at[1], rows, cols(k)],
            lambda k: w.at[src_at[0], src_at[1], rows, cols(k)],
            device,
            lambda k: w.at[land_at[0], land_at[1], rows, cols(k)],
            w.at[src_at[0], src_at[1], rows],
        )

    for half, rows in (("mine", mine), ("other", other)):
        piece_of("zp_" + half, dev_zp, (yl, z), (yl, zm), rows)
        piece_of("zm_" + half, dev_zm, (yl, z), (yl, zp), rows)
        piece_of("y_" + half, dev_y, (yl, z), (yo, z), rows)
    piece("far_zp", dev_zp, (yl, zm), (yl, z2), 0, CR // 2)
    piece("far_zm", dev_zm, (yl, zp), (yl, z2), CR // 2, CR // 2)
    piece("zm_y", dev_y, (yl, zm), (yo, zm), 0, G1)
    piece("zp_y", dev_y, (yl, zp), (yo, zp), 0, G1)
    piece("y_zp", dev_zp, (yo, z), (yo, zm), G1, G2)
    piece("y_zm", dev_zm, (yo, z), (yo, zp), G1, G2)
    piece("z2_y", dev_y, (yl, z2), (yo, z2), 0, G1)
    piece("yfar_zp", dev_zp, (yo, zm), (yo, z2), G1, GH)
    piece("yfar_zm", dev_zm, (yo, zp), (yo, z2), G1 + GH, GH)

    def ag_own(k, half):
        ag.start("zp_" + half, k)
        ag.start("zm_" + half, k)
        ag.start("y_" + half, k)

    def ag_a(k):
        ag_own(k, "mine")
        swap.arrived("w", k)
        ag_own(k, "other")

    def ag_b(k):
        ag.arrived("y_mine", k)
        ag.arrived("y_other", k)
        ag.start("y_zp", k)
        ag.start("y_zm", k)
        ag.arrived("zp_mine", k)
        ag.arrived("zp_other", k)
        ag.start("far_zp", k)
        ag.start("zm_y", k)
        ag.arrived("zm_mine", k)
        ag.arrived("zm_other", k)
        ag.start("far_zm", k)
        ag.start("zp_y", k)

    def ag_c(k):
        ag.arrived("far_zp", k)
        ag.start("z2_y", k)
        ag.arrived("y_zp", k)
        ag.start("yfar_zp", k)
        ag.arrived("y_zm", k)
        ag.start("yfar_zm", k)

    def ag_d(k):
        for name in ("far_zm", "zm_y", "zp_y", "z2_y", "yfar_zp", "yfar_zm"):
            ag.arrived(name, k)

    rs = Lane(rs_s, rs_r)
    rs.add("a_y", lambda k: g.at[yo, :, pl.ds(0, R1), cols(k)], lambda k: ry1.at[k], dev_y,
           lambda k: ry1.at[k], g.at[yo, :, pl.ds(0, R1)])
    rs.add("a_zp", lambda k: g.at[:, z2, pl.ds(R1, H2), cols(k)], lambda k: rf.at[0, k], dev_zp,
           lambda k: rf.at[0, k], g.at[:, z2, pl.ds(R1, H2)])
    rs.add("a_zm", lambda k: g.at[:, z2, pl.ds(R1 + H2, H2), cols(k)], lambda k: rf.at[1, k],
           dev_zm, lambda k: rf.at[1, k], g.at[:, z2, pl.ds(R1 + H2, H2)])
    rs.add("b1_zp", lambda k: g.at[yl, z2, pl.ds(0, H1), cols(k)], lambda k: rg.at[0, k], dev_zp,
           lambda k: rg.at[0, k], g.at[yl, z2, pl.ds(0, H1)])
    rs.add("b1_zm", lambda k: g.at[yl, z2, pl.ds(H1, H1), cols(k)], lambda k: rg.at[1, k], dev_zm,
           lambda k: rg.at[1, k], g.at[yl, z2, pl.ds(H1, H1)])
    rs.add("b2_zp", lambda k: g.at[:, zp, pl.ds(R1, R2), cols(k)], lambda k: rn.at[0, k], dev_zp,
           lambda k: rn.at[0, k], g.at[:, zp, pl.ds(R1, R2)])
    rs.add("b2_zm", lambda k: g.at[:, zm, pl.ds(R1, R2), cols(k)], lambda k: rn.at[1, k], dev_zm,
           lambda k: rn.at[1, k], g.at[:, zm, pl.ds(R1, R2)])
    rs.add("c_zp", lambda k: g.at[yl, zp, pl.ds(0, R1), cols(k)], lambda k: rm.at[0, k], dev_zp,
           lambda k: rm.at[0, k], g.at[yl, zp, pl.ds(0, R1)])
    rs.add("c_zm", lambda k: g.at[yl, zm, pl.ds(0, R1), cols(k)], lambda k: rm.at[1, k], dev_zm,
           lambda k: rm.at[1, k], g.at[yl, zm, pl.ds(0, R1)])
    rs.add("c_y", lambda k: g.at[yo, z, pl.ds(R1, R2), cols(k)], lambda k: ry2.at[k], dev_y,
           lambda k: ry2.at[k], g.at[yo, z, pl.ds(R1, R2)])

    def plus(first, *rest):
        total = first.astype(F32)
        for term in rest:
            total = total + term.astype(F32)
        return total

    def add_into(at, *terms):
        total = g[at]
        for term in terms:
            total = total + term
        g[at] = total

    def rs_a(k):
        rs.start("a_y", k)
        rs.start("a_zp", k)
        rs.start("a_zm", k)

    def rs_b(k):
        rs.arrived("a_zp", k)
        add_into((slice(None), zp, pl.ds(R1, H2), cols(k)), rf[0, k])
        rs.start("b2_zp", k)
        rs.arrived("a_zm", k)
        add_into((slice(None), zm, pl.ds(R1 + H2, H2), cols(k)), rf[1, k])
        rs.start("b2_zm", k)
        rs.arrived("a_y", k)
        add_into((yl, slice(None), pl.ds(0, R1), cols(k)), ry1[k])
        rs.start("b1_zp", k)
        rs.start("b1_zm", k)

    def rs_c(k):
        rs.arrived("b2_zp", k)
        rs.arrived("b2_zm", k)
        add_into((slice(None), z, pl.ds(R1, R2), cols(k)), rn[0, k], rn[1, k])
        rs.start("c_y", k)
        rs.arrived("b1_zp", k)
        add_into((yl, zp, pl.ds(0, H1), cols(k)), rg[0, k])
        rs.start("c_zp", k)
        rs.arrived("b1_zm", k)
        add_into((yl, zm, pl.ds(H1, H1), cols(k)), rg[1, k])
        rs.start("c_zm", k)

    def wg_local(k):
        return pltpu.make_async_copy(
            fin.at[mine, cols(k)], wg_out.at[:, wide_cols(c, k)], wg_sem.at[0, k]
        )

    def wg_remote(k, landed=False):
        target = wg_out.at[:, wide_cols((1 - c) if landed else c, k)]
        return pltpu.make_async_remote_copy(
            src_ref=fin.at[other, cols(k)],
            dst_ref=target,
            send_sem=wg_sem.at[1, k],
            recv_sem=wg_sem.at[2, k],
            device_id=dev_c,
            device_id_type=MESH,
        )

    def rs_d(k):
        rs.arrived("c_zp", k)
        rs.arrived("c_zm", k)
        fin[pl.ds(0, R1), cols(k)] = plus(g[yl, z, pl.ds(0, R1), cols(k)], rm[0, k], rm[1, k])
        rs.arrived("c_y", k)
        fin[pl.ds(R1, R2), cols(k)] = plus(g[yl, z, pl.ds(R1, R2), cols(k)], ry2[k])
        wg_local(k).start()
        wg_remote(k).start()

    def act_local(k):
        return pltpu.make_async_copy(
            act.at[pl.ds(0, TOK), cols(k)], act_out.at[:, wide_cols(c, k)], act_sem.at[0, k]
        )

    def act_remote(k, landed=False):
        return pltpu.make_async_remote_copy(
            src_ref=act.at[pl.ds(TOK, TOK), cols(k)],
            dst_ref=act_out.at[:, wide_cols((1 - c) if landed else c, k)],
            send_sem=act_sem.at[1, k],
            recv_sem=act_sem.at[2, k],
            device_id=dev_c,
            device_id_type=MESH,
        )

    def forward(k, count):
        at = pl.ds(pl.multiple_of(k * BLK, BLK), count * BLK)

        @pl.loop(0, 4)
        def _(t):
            rows = pl.ds(pl.multiple_of(t * 256, 256), 256)
            weight = w[:, :, :, at].reshape(D, count * BLK)
            preact = jnp.dot(normed[rows], weight, preferred_element_type=F32)
            sig = 1.0 / (1.0 + jnp.exp(-preact))
            act[rows, at] = (preact * sig).astype(BF16)
            grad = (pg[rows, at].astype(F32) * sig * (1.0 + preact * (1.0 - sig))).astype(BF16)
            pg[rows, at] = grad
            dots = preact * grad.astype(F32)
            for i in range(count):
                rdacc[rows] += dots[:, i * BLK : (i + 1) * BLK]

        for i in range(count):
            act_local(k + i).start()
            act_remote(k + i).start()

    def weight_part(k):
        turned = pg[:, cols(k)].T
        for q in range(8):
            part = jnp.dot(turned, normed[:, q * CR : (q + 1) * CR], preferred_element_type=F32)
            g[q // 4, q % 4, :, cols(k)] = part.T.astype(BF16)

    xs = Lane(x_s, x_r)

    def span(start, n):
        return pl.ds(pl.multiple_of(start, BLK), n)

    xs.add("far_p", lambda j: ng.at[trows(j), span(x2 * XS, WS)], lambda j: xf.at[0, trows(j)],
           dev_xp, lambda j: xf.at[0, trows(j)], ng.at[pl.ds(0, TOK), span(0, WS)])
    xs.add("far_m", lambda j: ng.at[trows(j), span(x2 * XS + WS, WS)], lambda j: xf.at[1, trows(j)],
           dev_xm, lambda j: xf.at[1, trows(j)], ng.at[pl.ds(0, TOK), span(0, WS)])
    xs.add("near_p", lambda j: ng.at[trows(j), span(xp * XS, XS)], lambda j: xn.at[0, trows(j)],
           dev_xp, lambda j: xn.at[0, trows(j)], ng.at[pl.ds(0, TOK), span(0, XS)])
    xs.add("near_m", lambda j: ng.at[trows(j), span(xm * XS, XS)], lambda j: xn.at[1, trows(j)],
           dev_xm, lambda j: xn.at[1, trows(j)], ng.at[pl.ds(0, TOK), span(0, XS)])
    xs.add("h", lambda j: hs.at[trows(j)], lambda j: hr.at[trows(j)], dev_h,
           lambda j: hr.at[trows(j)], hs)

    def quarter(i):
        m, n = i // 2, i % 2
        return (x + 2 - n + m * (1 - 2 * n)) % 4

    sib = Lane(si_s, si_r)
    sib.add(
        "s",
        lambda i: ng.at[pl.ds(TOK, TOK), span(quarter(i) * XS, XS)],
        lambda i: nr.at[:, span(quarter(i) * XS, XS)],
        dev_c,
        lambda i: nr.at[:, span(quarter(i) * XS, XS)],
        nr,
    )

    def grads_times_weight(i, t, lo, n, first):
        rows = pl.ds(pl.multiple_of((1 - t) * TOK, TOK), TOK)
        for h in range(2):
            block = quarter(i) * 2 + h
            part = lax.dot_general(
                pg[rows, lo : lo + n],
                w[block // 4, block % 4, :, lo : lo + n],
                (((1,), (1,)), ((), ())),
                preferred_element_type=F32,
            )
            at = (rows, span(block * CR, CR))
            ng[at] = part.astype(BF16) if first else plus(part, ng[at]).astype(BF16)

    def ng_first(i):
        @pl.loop(0, 2)
        def _(t):
            grads_times_weight(i, t, 0, KP, True)

    def ng_p(i):
        @pl.loop(0, 2)
        def _(t):
            grads_times_weight(i, t, KP, HALF - KP, False)

            @pl.when(t == 0)
            def _():
                sib.start("s", i)

    def ng_q():
        sib.arrived("s", 0)

        @pl.loop(0, NB)
        def _(j):
            at = (trows(j), span(x2 * XS, XS))
            ng[at] = ng[at] + nr[at]
            xs.start("far_p", j)
            xs.start("far_m", j)

    def sibs_here():
        for i in range(1, 4):
            sib.arrived("s", i)

    def ng_r(j):
        low, high = (trows(j), span(xp * XS, WS)), (trows(j), span(xp * XS + WS, WS))
        xs.arrived("far_p", j)
        ng[low] = ng[low] + nr[low] + xf[0, trows(j)]
        ng[high] = ng[high] + nr[high]
        xs.start("near_p", j)
        low, high = (trows(j), span(xm * XS, WS)), (trows(j), span(xm * XS + WS, WS))
        xs.arrived("far_m", j)
        ng[high] = ng[high] + nr[high] + xf[1, trows(j)]
        ng[low] = ng[low] + nr[low]
        xs.start("near_m", j)

    def ng_u(j):
        xs.arrived("near_p", j)
        xs.arrived("near_m", j)
        theirs, ours = span((1 - yh) * WS, WS), span(yh * WS, WS)
        base = x * XS
        for half, at in ((theirs, base + (1 - yh) * WS), (ours, base + yh * WS)):
            total = plus(
                ng[trows(j), span(at, WS)],
                nr[trows(j), span(at, WS)],
                xn[0, trows(j), half],
                xn[1, trows(j), half],
            )
            if half is theirs:
                hs[trows(j)] = total.astype(BF16)
                xs.start("h", j)
            else:
                ho[trows(j)] = total

    def ig_copy(j):
        return pltpu.make_async_copy(igv.at[trows(j)], ig_out.at[trows(j)], ig_sem.at[j])

    def ng_v(j):
        xs.arrived("h", j)
        scaled = plus(ho[trows(j)], hr[trows(j)]) * gain[:, span(wi * WS, WS)]
        scale = inv[trows(j)][:, :1]
        dots = rdacc[trows(j)][:, :1]
        igv[trows(j)] = (scale * scaled - tsl[trows(j)].astype(F32) * (scale * scale) * dots).astype(
            BF16
        )
        ig_copy(j).start()

    rds = Lane(rd_s, rd_r)
    rds.add("s", lambda k: rdo.at[1], lambda k: rdr, dev_c, lambda k: rdr, rdr)
    rws = Lane(rw_s, rw_r)
    for r in range(7):
        rws.add(str(r), lambda k: rdo.at[0], lambda k, r=r: rdw.at[r], dev_w[r],
                lambda k, r=r: rdw.at[r], rdr)

    def rd_1():
        ones = jnp.ones((8, BLK), F32)
        for half in range(2):
            rdo[half] = lax.dot_general(
                ones,
                rdacc[half * TOK : (half + 1) * TOK],
                (((1,), (1,)), ((), ())),
                precision=lax.Precision.HIGHEST,
                preferred_element_type=F32,
            )
        rds.start("s", 0)

    def rd_2():
        rds.arrived("s", 0)
        rdo[0] = rdo[0] + rdr[...]
        for r in range(7):
            rws.start(str(r), 0)

    def rd_3():
        load_tsl.wait()
        for r in range(7):
            rws.arrived(str(r), 0)
        total = rdo[0]
        for r in range(7):
            total = total + rdw[r]
        rdacc[pl.ds(0, TOK)] = jnp.broadcast_to((total / D).T[:, :1], (TOK, BLK))

    rotation = hadamard()

    def decoded(core, k):
        at = wide_cols(core, k)
        turned = jnp.dot(cod[:, at], rotation, preferred_element_type=F32)
        block = core * CH + k
        norm = 1.0 / (BLK**0.5)
        top = turned[:BLK] * (grid[codes[0, block]] * norm)
        low = turned[BLK:] * (grid[codes[1, block]] * norm)
        return jnp.concatenate([top, low], axis=0).astype(BF16)

    def decode(k):
        wsib[:, cols(k)] = decoded(1 - c, k)
        swap.start("w", k)
        w[yl, z, mine, cols(k)] = decoded(c, k)

    decode(0)
    ag_own(0, "mine")

    @pl.loop(1, CH)
    def _(k):
        decode(k)

    swap.arrived("w", 0)
    ag_own(0, "other")
    for i in range(1, LA):
        ag_a(i)

    cts.start("c", 0)

    def norm_tokens():
        rdacc[...] = jnp.zeros_like(rdacc)
        load_tok.wait()

        @pl.loop(0, NB)
        def _(j):
            @pl.loop(0, TB // 32)
            def _(i):
                rows = pl.ds(pl.multiple_of(j * TB + i * 32, 32), 32)
                values = ng[rows].astype(F32)
                scale = lax.rsqrt(
                    jnp.sum(values * values, axis=-1, keepdims=True) * (1.0 / D) + 1e-5
                )
                inv[rows] = jnp.broadcast_to(scale, (32, BLK))
                normed[rows] = (values * scale * gain[...]).astype(BF16)

            nms.start("n", j)

        load_cot.wait()

    def inputs_here():
        cts.arrived("c", 0)
        @pl.loop(0, NB)
        def _(j):
            nms.arrived("n", j)

    def at_step(s, fn, first, count, each=1):
        @pl.when((s >= first) & (s < first + count // each))
        def _():
            if each == 1:
                fn(s - first)
            else:

                @pl.loop(0, each)
                def _(i):
                    fn((s - first) * each + i)

    def once(s, fn, step):
        @pl.when(s == step)
        def _():
            fn()

    def several(fn, k, count):
        @pl.loop(0, count)
        def _(i):
            fn(k + i)

    done = CH - 1 + LD

    @pl.loop(0, STEPS)
    def _(s):
        at_step(s, lambda k: ag_a(k + LA), 0, CH - LA)
        at_step(s, ag_b, 0, CH)
        at_step(s, ag_c, LC, CH)
        once(s, norm_tokens, 0)
        once(s, inputs_here, LD)
        once(s, lambda: several(rs_a, 0, RE), CH - 1)
        once(s, lambda: several(rs_a, RE, 4 - RE), CH)
        once(s, lambda: several(weight_part, 5, 2), done + 1)
        once(s, lambda: several(rs_a, 4, 3), done + 1)
        at_step(s, lambda k: rs_b(k + 2), done + 1, CH - 2)
        once(s, sibs_here, done + NR)
        at_step(s, ng_r, done + NR, NB, ER)
        at_step(s, rs_c, done + RC, CH)
        at_step(s, ng_u, done + NU, NB, EU)
        once(s, rd_1, done + 2)
        once(s, rd_2, done + 3)
        once(s, rd_3, done + 4)
        at_step(s, ng_v, done + NV, NB, EU)
        at_step(s, rs_d, done + RD, CH)
        once(s, lambda: several(weight_part, 0, 2), LD + 2)
        once(s, lambda: several(weight_part, 2, 2), LD + 4)
        at_step(s, ag_d, LD, CH)

        @pl.when((s > LD) & (s < done) & ((s - LD) % 2 == 1))
        def _():
            forward(s - LD - 1, 2)

        at_step(s, ng_first, LD + 3, 4, 2)
        once(s, lambda: weight_part(4), CH)
        once(s, lambda: forward(CH - 1, 1), done)

        @pl.when(s == done)
        def _():
            @pl.loop(0, 2)
            def _(i):
                rs_b(i)
                several(ng_p, 2 * i, 2)

            ng_q()

    for lane in (swap, ag, rs, nms, xs, sib, cts, rds, rws):
        lane.drain()

    @pl.loop(0, CH)
    def _(k):
        act_local(k).wait()
        act_remote(k).wait_send()
        act_remote(k, True).wait_recv()
        wg_local(k).wait()
        wg_remote(k).wait_send()
        wg_remote(k, True).wait_recv()

    @pl.loop(0, NB)
    def _(j):
        ig_copy(j).wait()


def hand_over(act, wg, ig, act_out, wg_out, ig_out, act_v, wg_v, ig_v, sems):
    loads, stores = [], []
    for i, (src, mid, dst) in enumerate(
        ((act, act_v, act_out), (wg, wg_v, wg_out), (ig, ig_v, ig_out))
    ):
        rows = src.shape[0] // PARTS
        for part in range(PARTS):
            at = pl.ds(part * rows, rows)
            loads.append(pltpu.make_async_copy(src.at[at], mid.at[at], sems.at[0, i, part]))
            stores.append(pltpu.make_async_copy(mid.at[at], dst.at[at], sems.at[1, i, part]))
    for load in loads:
        load.start()
    for load, store in zip(loads, stores):
        load.wait()
        store.start()
    for store in stores:
        store.wait()


def per_device(tokens, norm_gain, coded, block_codes, grid, cotangent):
    anywhere = pl.BlockSpec(memory_space=pl.ANY)
    vmem = pl.BlockSpec(memory_space=pltpu.VMEM)
    smem = pl.BlockSpec(memory_space=pltpu.SMEM)
    sem = pltpu.SemaphoreType.DMA
    results = pl.pallas_call(
        kernel,
        out_shape=(
            jax.ShapeDtypeStruct((TOK, CW), BF16),
            jax.ShapeDtypeStruct((D // 16, CW), F32),
            jax.ShapeDtypeStruct((TOK, WS), BF16),
        ),
        in_specs=[anywhere, vmem, anywhere, smem, smem, anywhere],
        out_specs=(anywhere, anywhere, anywhere),
        scratch_shapes=[
            pltpu.VMEM((256, CW), BF16),
            pltpu.VMEM((256, HALF), BF16),
            pltpu.VMEM((2, 4, CR, HALF), BF16),
            pltpu.VMEM((2 * TOK, D), BF16),
            pltpu.VMEM((2 * TOK, HALF), BF16),
            pltpu.VMEM((2 * TOK, HALF), BF16),
            pltpu.VMEM((2, 4, CR, HALF), BF16),
            pltpu.VMEM((CR, HALF), F32),
            pltpu.VMEM((2 * TOK, D), BF16),
            pltpu.VMEM((TOK, D), BF16),
            pltpu.VMEM((2, TOK, WS), BF16),
            pltpu.VMEM((2, TOK, XS), BF16),
            pltpu.VMEM((TOK, WS), BF16),
            pltpu.VMEM((TOK, WS), BF16),
            pltpu.VMEM((TOK, WS), F32),
            pltpu.VMEM((TOK, WS), BF16),
            pltpu.VMEM((TOK, WS), BF16),
            pltpu.VMEM((TOK, BLK), F32),
            pltpu.VMEM((2 * TOK, BLK), F32),
            pltpu.VMEM((2, 8, TOK), F32),
            pltpu.VMEM((8, TOK), F32),
            pltpu.VMEM((7, 8, TOK), F32),
            pltpu.VMEM((CH, 4, R1, BLK), BF16),
            pltpu.VMEM((2, CH, 2, H2, BLK), BF16),
            pltpu.VMEM((2, CH, H1, BLK), BF16),
            pltpu.VMEM((2, CH, 2, R2, BLK), BF16),
            pltpu.VMEM((2, CH, R1, BLK), BF16),
            pltpu.VMEM((CH, R2, BLK), BF16),
            sem((4,)), sem((3, CH)), sem((3, CH)), sem((NB,)),
            sem((15,)), sem((15, CH)), sem((10,)), sem((10, CH)), sem((1,)), sem((1, 4)),
            sem((1,)), sem((1, CH)), sem((1,)), sem((1, NB)), sem((5,)), sem((5, NB)),
            sem((1,)), sem((1, 1)), sem((7,)), sem((7, 1)), sem((1,)), sem((1, 1)),
        ],
        compiler_params=pltpu.CompilerParams(
            collective_id=0, has_side_effects=True, vmem_limit_bytes=63 << 20
        ),
        cost_estimate=pl.CostEstimate(
            flops=6 * TOK * D * CW, bytes_accessed=40 << 20, transcendentals=TOK * CW
        ),
    )(tokens, norm_gain.reshape(1, D), coded, block_codes, grid, cotangent)
    return pl.pallas_call(
        hand_over,
        out_shape=tuple(jax.ShapeDtypeStruct(r.shape, r.dtype) for r in results),
        in_specs=[anywhere] * 3,
        out_specs=(anywhere,) * 3,
        scratch_shapes=[pltpu.VMEM(r.shape, r.dtype) for r in results] + [sem((2, 3, PARTS))],
        compiler_params=pltpu.CompilerParams(vmem_limit_bytes=63 << 20),
    )(*results)


def solution(mesh):
    placed = (
        P("narrow", None), P(), P("narrow", "wide"), P("narrow", "wide"), P(), P("narrow", "wide"),
    )
    return jax.shard_map(
        per_device,
        mesh=mesh,
        in_specs=placed,
        out_specs=(P("narrow", "wide"), P("narrow", "wide"), P("narrow", "wide")),
        check_vma=False,
    )
```

```python
import jax
import jax.numpy as jnp
from jax import lax
from jax.experimental import pallas as pl
from jax.experimental.pallas import tpu as pltpu
from jax.sharding import PartitionSpec as P

MESH = pl.DeviceIdType.MESH
F32, BF16 = jnp.float32, jnp.bfloat16

D = 4096
TOK = 512
CW = 1792
HALF = 896
BLK = 128
CH = HALF // BLK
CR = 512
G1 = 224
G2, GH = CR - G1, (CR - G1) // 2
R1 = 160
R2 = CR - R1
H1, H2 = R1 // 2, R2 // 2
KP = 4 * BLK
NB = 8
TB = TOK // NB
XS = D // 4
WS = D // 8

LA, LC, LD = 1, 1, 2
RC, RD = 1, 3
RE = 1
NR, NU, NV = 2, 3, 5
ER, EU = 2, 2
PARTS = 2
STEPS = CH - 1 + LD + max(CH + RD, NV + NB // EU)


def hadamard():
    both = lax.broadcasted_iota(jnp.int32, (BLK, BLK), 0) & lax.broadcasted_iota(
        jnp.int32, (BLK, BLK), 1
    )
    for shift in (4, 2, 1):
        both = both ^ lax.shift_right_logical(both, shift)
    return (1 - 2 * (both & 1)).astype(F32).astype(BF16)


class Lane:
    def __init__(self, send_sems, recv_sems):
        self.send_sems, self.recv_sems, self.kinds, self.rows = send_sems, recv_sems, {}, {}

    def add(self, name, src, dst, device, land, whole):
        self.rows[name] = len(self.kinds)
        self.kinds[name] = (src, dst, device, land, whole)

    def copy(self, name, k, src, dst):
        row = self.rows[name]
        return pltpu.make_async_remote_copy(
            src_ref=src,
            dst_ref=dst,
            send_sem=self.send_sems.at[row],
            recv_sem=self.recv_sems.at[row, k],
            device_id=self.kinds[name][2],
            device_id_type=MESH,
        )

    def start(self, name, k):
        src, dst, _, _, _ = self.kinds[name]
        self.copy(name, k, src(k), dst(k)).start()

    def arrived(self, name, k):
        land = self.kinds[name][3]
        self.copy(name, k, land(k), land(k)).wait_recv()

    def drain(self):
        for name, (_, _, _, _, whole) in self.kinds.items():
            self.copy(name, 0, whole, whole).wait_send()


def kernel(
    tokens, gain, coded, codes, grid, cot,
    act_out, wg_out, ig_out,
    cod, wsib, w, normed, pg, act, g, fin,
    ng, nr, xf, xn, hs, hr, ho, tsl, igv,
    inv, rdacc, rdo, rdr, rdw,
    ry1, rf, rg, rn, rm, ry2,
    loc, act_sem, wg_sem, ig_sem,
    ag_s, ag_r, rs_s, rs_r, si_s, si_r, sw_s, sw_r, nm_s, nm_r, x_s, x_r, rd_s, rd_r, rw_s, rw_r, ct_s, ct_r,
):
    wi, ni = lax.axis_index("wide"), lax.axis_index("narrow")
    x, yh = wi // 2, wi % 2
    yl, z, c = ni // 8, (ni // 2) % 4, ni % 2
    zp, zm, z2 = (z + 1) % 4, (z + 3) % 4, (z + 2) % 4
    xp, xm, x2 = (x + 1) % 4, (x + 3) % 4, (x + 2) % 4
    yo = 1 - yl
    dev_zp = (wi, (yl * 4 + zp) * 2 + c)
    dev_zm = (wi, (yl * 4 + zm) * 2 + c)
    dev_y = (wi, (yo * 4 + z) * 2 + c)
    dev_c = (wi, (yl * 4 + z) * 2 + (1 - c))
    dev_xp = (xp * 2 + yh, ni)
    dev_xm = (xm * 2 + yh, ni)
    dev_h = (x * 2 + (1 - yh), ni)
    dev_w = [((wi + r) % 8, ni) for r in range(1, 8)]

    def cols(k):
        return pl.ds(pl.multiple_of(k * BLK, BLK), BLK)

    def wide_cols(core, k):
        return pl.ds(pl.multiple_of(core * HALF + k * BLK, BLK), BLK)

    def trows(j, base=0):
        return pl.ds(pl.multiple_of(base + j * TB, TB), TB)

    mine = pl.ds(pl.multiple_of(c * 256, 256), 256)
    other = pl.ds(pl.multiple_of((1 - c) * 256, 256), 256)

    load_cod = pltpu.make_async_copy(coded, cod, loc.at[0])
    load_tok = pltpu.make_async_copy(tokens, ng.at[pl.ds(0, TOK)], loc.at[1])
    load_cot = pltpu.make_async_copy(
        cot.at[:, pl.ds(pl.multiple_of(c * HALF, BLK), HALF)], pg.at[pl.ds(0, TOK)], loc.at[2]
    )
    load_tsl = pltpu.make_async_copy(
        tokens.at[:, pl.ds(pl.multiple_of(wi * WS, BLK), WS)], tsl, loc.at[3]
    )
    load_cod.start()
    barrier = pltpu.get_barrier_semaphore()
    partners = [dev_zp, dev_zm, dev_y, dev_c, *dev_w]
    for device in partners:
        pl.semaphore_signal(barrier, inc=1, device_id=device, device_id_type=MESH)
    load_tok.start()
    load_cot.start()
    load_tsl.start()
    load_cod.wait()
    pl.semaphore_wait(barrier, len(partners))

    swap = Lane(sw_s, sw_r)
    swap.add(
        "w",
        lambda k: wsib.at[:, cols(k)],
        lambda k: w.at[yl, z, mine, cols(k)],
        dev_c,
        lambda k: w.at[yl, z, other, cols(k)],
        wsib,
    )
    cts = Lane(ct_s, ct_r)
    cts.add(
        "c",
        lambda k: cot.at[:, pl.ds(pl.multiple_of((1 - c) * HALF, BLK), HALF)],
        lambda k: pg.at[pl.ds(TOK, TOK)],
        dev_c,
        lambda k: pg.at[pl.ds(TOK, TOK)],
        pg.at[pl.ds(TOK, TOK)],
    )
    nms = Lane(nm_s, nm_r)
    nms.add(
        "n",
        lambda j: normed.at[trows(j)],
        lambda j: normed.at[trows(j, TOK)],
        dev_c,
        lambda j: normed.at[trows(j, TOK)],
        normed.at[pl.ds(TOK, TOK)],
    )

    ag = Lane(ag_s, ag_r)

    def piece(name, device, src_at, land_at, lo, n):
        piece_of(name, device, src_at, land_at, pl.ds(lo, n))

    def piece_of(name, device, src_at, land_at, rows):
        ag.add(
            name,
            lambda k: w.at[src_at[0], src_at[1], rows, cols(k)],
            lambda k: w.at[src_at[0], src_at[1], rows, cols(k)],
            device,
            lambda k: w.at[land_at[0], land_at[1], rows, cols(k)],
            w.at[src_at[0], src_at[1], rows],
        )

    for half, rows in (("mine", mine), ("other", other)):
        piece_of("zp_" + half, dev_zp, (yl, z), (yl, zm), rows)
        piece_of("zm_" + half, dev_zm, (yl, z), (yl, zp), rows)
        piece_of("y_" + half, dev_y, (yl, z), (yo, z), rows)
    piece("far_zp", dev_zp, (yl, zm), (yl, z2), 0, CR // 2)
    piece("far_zm", dev_zm, (yl, zp), (yl, z2), CR // 2, CR // 2)
    piece("zm_y", dev_y, (yl, zm), (yo, zm), 0, G1)
    piece("zp_y", dev_y, (yl, zp), (yo, zp), 0, G1)
    piece("y_zp", dev_zp, (yo, z), (yo, zm), G1, G2)
    piece("y_zm", dev_zm, (yo, z), (yo, zp), G1, G2)
    piece("z2_y", dev_y, (yl, z2), (yo, z2), 0, G1)
    piece("yfar_zp", dev_zp, (yo, zm), (yo, z2), G1, GH)
    piece("yfar_zm", dev_zm, (yo, zp), (yo, z2), G1 + GH, GH)

    def ag_own(k, half):
        ag.start("zp_" + half, k)
        ag.start("zm_" + half, k)
        ag.start("y_" + half, k)

    def ag_a(k):
        ag_own(k, "mine")
        swap.arrived("w", k)
        ag_own(k, "other")

    def ag_b(k):
        ag.arrived("y_mine", k)
        ag.arrived("y_other", k)
        ag.start("y_zp", k)
        ag.start("y_zm", k)
        ag.arrived("zp_mine", k)
        ag.arrived("zp_other", k)
        ag.start("far_zp", k)
        ag.start("zm_y", k)
        ag.arrived("zm_mine", k)
        ag.arrived("zm_other", k)
        ag.start("far_zm", k)
        ag.start("zp_y", k)

    def ag_c(k):
        ag.arrived("far_zp", k)
        ag.start("z2_y", k)
        ag.arrived("y_zp", k)
        ag.start("yfar_zp", k)
        ag.arrived("y_zm", k)
        ag.start("yfar_zm", k)

    def ag_d(k):
        for name in ("far_zm", "zm_y", "zp_y", "z2_y", "yfar_zp", "yfar_zm"):
            ag.arrived(name, k)

    rs = Lane(rs_s, rs_r)
    rs.add("a_y", lambda k: g.at[yo, :, pl.ds(0, R1), cols(k)], lambda k: ry1.at[k], dev_y,
           lambda k: ry1.at[k], g.at[yo, :, pl.ds(0, R1)])
    rs.add("a_zp", lambda k: g.at[:, z2, pl.ds(R1, H2), cols(k)], lambda k: rf.at[0, k], dev_zp,
           lambda k: rf.at[0, k], g.at[:, z2, pl.ds(R1, H2)])
    rs.add("a_zm", lambda k: g.at[:, z2, pl.ds(R1 + H2, H2), cols(k)], lambda k: rf.at[1, k],
           dev_zm, lambda k: rf.at[1, k], g.at[:, z2, pl.ds(R1 + H2, H2)])
    rs.add("b1_zp", lambda k: g.at[yl, z2, pl.ds(0, H1), cols(k)], lambda k: rg.at[0, k], dev_zp,
           lambda k: rg.at[0, k], g.at[yl, z2, pl.ds(0, H1)])
    rs.add("b1_zm", lambda k: g.at[yl, z2, pl.ds(H1, H1), cols(k)], lambda k: rg.at[1, k], dev_zm,
           lambda k: rg.at[1, k], g.at[yl, z2, pl.ds(H1, H1)])
    rs.add("b2_zp", lambda k: g.at[:, zp, pl.ds(R1, R2), cols(k)], lambda k: rn.at[0, k], dev_zp,
           lambda k: rn.at[0, k], g.at[:, zp, pl.ds(R1, R2)])
    rs.add("b2_zm", lambda k: g.at[:, zm, pl.ds(R1, R2), cols(k)], lambda k: rn.at[1, k], dev_zm,
           lambda k: rn.at[1, k], g.at[:, zm, pl.ds(R1, R2)])
    rs.add("c_zp", lambda k: g.at[yl, zp, pl.ds(0, R1), cols(k)], lambda k: rm.at[0, k], dev_zp,
           lambda k: rm.at[0, k], g.at[yl, zp, pl.ds(0, R1)])
    rs.add("c_zm", lambda k: g.at[yl, zm, pl.ds(0, R1), cols(k)], lambda k: rm.at[1, k], dev_zm,
           lambda k: rm.at[1, k], g.at[yl, zm, pl.ds(0, R1)])
    rs.add("c_y", lambda k: g.at[yo, z, pl.ds(R1, R2), cols(k)], lambda k: ry2.at[k], dev_y,
           lambda k: ry2.at[k], g.at[yo, z, pl.ds(R1, R2)])

    def plus(first, *rest):
        total = first.astype(F32)
        for term in rest:
            total = total + term.astype(F32)
        return total

    def add_into(at, *terms):
        total = g[at]
        for term in terms:
            total = total + term
        g[at] = total

    def rs_a(k):
        rs.start("a_y", k)
        rs.start("a_zp", k)
        rs.start("a_zm", k)

    def rs_b(k):
        rs.arrived("a_zp", k)
        add_into((slice(None), zp, pl.ds(R1, H2), cols(k)), rf[0, k])
        rs.start("b2_zp", k)
        rs.arrived("a_zm", k)
        add_into((slice(None), zm, pl.ds(R1 + H2, H2), cols(k)), rf[1, k])
        rs.start("b2_zm", k)
        rs.arrived("a_y", k)
        add_into((yl, slice(None), pl.ds(0, R1), cols(k)), ry1[k])
        rs.start("b1_zp", k)
        rs.start("b1_zm", k)

    def rs_c(k):
        rs.arrived("b2_zp", k)
        rs.arrived("b2_zm", k)
        add_into((slice(None), z, pl.ds(R1, R2), cols(k)), rn[0, k], rn[1, k])
        rs.start("c_y", k)
        rs.arrived("b1_zp", k)
        add_into((yl, zp, pl.ds(0, H1), cols(k)), rg[0, k])
        rs.start("c_zp", k)
        rs.arrived("b1_zm", k)
        add_into((yl, zm, pl.ds(H1, H1), cols(k)), rg[1, k])
        rs.start("c_zm", k)

    def wg_local(k):
        return pltpu.make_async_copy(
            fin.at[mine, cols(k)], wg_out.at[:, wide_cols(c, k)], wg_sem.at[0, k]
        )

    def wg_remote(k, landed=False):
        target = wg_out.at[:, wide_cols((1 - c) if landed else c, k)]
        return pltpu.make_async_remote_copy(
            src_ref=fin.at[other, cols(k)],
            dst_ref=target,
            send_sem=wg_sem.at[1, k],
            recv_sem=wg_sem.at[2, k],
            device_id=dev_c,
            device_id_type=MESH,
        )

    def rs_d(k):
        rs.arrived("c_zp", k)
        rs.arrived("c_zm", k)
        fin[pl.ds(0, R1), cols(k)] = plus(g[yl, z, pl.ds(0, R1), cols(k)], rm[0, k], rm[1, k])
        rs.arrived("c_y", k)
        fin[pl.ds(R1, R2), cols(k)] = plus(g[yl, z, pl.ds(R1, R2), cols(k)], ry2[k])
        wg_local(k).start()
        wg_remote(k).start()

    def act_local(k):
        return pltpu.make_async_copy(
            act.at[pl.ds(0, TOK), cols(k)], act_out.at[:, wide_cols(c, k)], act_sem.at[0, k]
        )

    def act_remote(k, landed=False):
        return pltpu.make_async_remote_copy(
            src_ref=act.at[pl.ds(TOK, TOK), cols(k)],
            dst_ref=act_out.at[:, wide_cols((1 - c) if landed else c, k)],
            send_sem=act_sem.at[1, k],
            recv_sem=act_sem.at[2, k],
            device_id=dev_c,
            device_id_type=MESH,
        )

    def forward(k, count):
        at = pl.ds(pl.multiple_of(k * BLK, BLK), count * BLK)

        @pl.loop(0, 4)
        def _(t):
            rows = pl.ds(pl.multiple_of(t * 256, 256), 256)
            weight = w[:, :, :, at].reshape(D, count * BLK)
            preact = jnp.dot(normed[rows], weight, preferred_element_type=F32)
            sig = 1.0 / (1.0 + jnp.exp(-preact))
            act[rows, at] = (preact * sig).astype(BF16)
            grad = (pg[rows, at].astype(F32) * sig * (1.0 + preact * (1.0 - sig))).astype(BF16)
            pg[rows, at] = grad
            dots = preact * grad.astype(F32)
            for i in range(count):
                rdacc[rows] += dots[:, i * BLK : (i + 1) * BLK]

        for i in range(count):
            act_local(k + i).start()
            act_remote(k + i).start()

    def weight_part(k):
        turned = pg[:, cols(k)].T
        for q in range(8):
            part = jnp.dot(turned, normed[:, q * CR : (q + 1) * CR], preferred_element_type=F32)
            g[q // 4, q % 4, :, cols(k)] = part.T.astype(BF16)

    xs = Lane(x_s, x_r)

    def span(start, n):
        return pl.ds(pl.multiple_of(start, BLK), n)

    xs.add("far_p", lambda j: ng.at[trows(j), span(x2 * XS, WS)], lambda j: xf.at[0, trows(j)],
           dev_xp, lambda j: xf.at[0, trows(j)], ng.at[pl.ds(0, TOK), span(0, WS)])
    xs.add("far_m", lambda j: ng.at[trows(j), span(x2 * XS + WS, WS)], lambda j: xf.at[1, trows(j)],
           dev_xm, lambda j: xf.at[1, trows(j)], ng.at[pl.ds(0, TOK), span(0, WS)])
    xs.add("near_p", lambda j: ng.at[trows(j), span(xp * XS, XS)], lambda j: xn.at[0, trows(j)],
           dev_xp, lambda j: xn.at[0, trows(j)], ng.at[pl.ds(0, TOK), span(0, XS)])
    xs.add("near_m", lambda j: ng.at[trows(j), span(xm * XS, XS)], lambda j: xn.at[1, trows(j)],
           dev_xm, lambda j: xn.at[1, trows(j)], ng.at[pl.ds(0, TOK), span(0, XS)])
    xs.add("h", lambda j: hs.at[trows(j)], lambda j: hr.at[trows(j)], dev_h,
           lambda j: hr.at[trows(j)], hs)

    def quarter(i):
        m, n = i // 2, i % 2
        return (x + 2 - n + m * (1 - 2 * n)) % 4

    sib = Lane(si_s, si_r)
    sib.add(
        "s",
        lambda i: ng.at[pl.ds(TOK, TOK), span(quarter(i) * XS, XS)],
        lambda i: nr.at[:, span(quarter(i) * XS, XS)],
        dev_c,
        lambda i: nr.at[:, span(quarter(i) * XS, XS)],
        nr,
    )

    def grads_times_weight(i, t, lo, n, first):
        rows = pl.ds(pl.multiple_of((1 - t) * TOK, TOK), TOK)
        for h in range(2):
            block = quarter(i) * 2 + h
            part = lax.dot_general(
                pg[rows, lo : lo + n],
                w[block // 4, block % 4, :, lo : lo + n],
                (((1,), (1,)), ((), ())),
                preferred_element_type=F32,
            )
            at = (rows, span(block * CR, CR))
            ng[at] = part.astype(BF16) if first else plus(part, ng[at]).astype(BF16)

    def ng_first(i):
        @pl.loop(0, 2)
        def _(t):
            grads_times_weight(i, t, 0, KP, True)

    def ng_p(i):
        @pl.loop(0, 2)
        def _(t):
            grads_times_weight(i, t, KP, HALF - KP, False)

            @pl.when(t == 0)
            def _():
                sib.start("s", i)

    def ng_q():
        sib.arrived("s", 0)

        @pl.loop(0, NB)
        def _(j):
            at = (trows(j), span(x2 * XS, XS))
            ng[at] = ng[at] + nr[at]
            xs.start("far_p", j)
            xs.start("far_m", j)

    def sibs_here():
        for i in range(1, 4):
            sib.arrived("s", i)

    def ng_r(j):
        low, high = (trows(j), span(xp * XS, WS)), (trows(j), span(xp * XS + WS, WS))
        xs.arrived("far_p", j)
        ng[low] = ng[low] + nr[low] + xf[0, trows(j)]
        ng[high] = ng[high] + nr[high]
        xs.start("near_p", j)
        low, high = (trows(j), span(xm * XS, WS)), (trows(j), span(xm * XS + WS, WS))
        xs.arrived("far_m", j)
        ng[high] = ng[high] + nr[high] + xf[1, trows(j)]
        ng[low] = ng[low] + nr[low]
        xs.start("near_m", j)

    def ng_u(j):
        xs.arrived("near_p", j)
        xs.arrived("near_m", j)
        theirs, ours = span((1 - yh) * WS, WS), span(yh * WS, WS)
        base = x * XS
        for half, at in ((theirs, base + (1 - yh) * WS), (ours, base + yh * WS)):
            total = plus(
                ng[trows(j), span(at, WS)],
                nr[trows(j), span(at, WS)],
                xn[0, trows(j), half],
                xn[1, trows(j), half],
            )
            if half is theirs:
                hs[trows(j)] = total.astype(BF16)
                xs.start("h", j)
            else:
                ho[trows(j)] = total

    def ig_copy(j):
        return pltpu.make_async_copy(igv.at[trows(j)], ig_out.at[trows(j)], ig_sem.at[j])

    def ng_v(j):
        xs.arrived("h", j)
        scaled = plus(ho[trows(j)], hr[trows(j)]) * gain[:, span(wi * WS, WS)]
        scale = inv[trows(j)][:, :1]
        dots = rdacc[trows(j)][:, :1]
        igv[trows(j)] = (scale * scaled - tsl[trows(j)].astype(F32) * (scale * scale) * dots).astype(
            BF16
        )
        ig_copy(j).start()

    rds = Lane(rd_s, rd_r)
    rds.add("s", lambda k: rdo.at[1], lambda k: rdr, dev_c, lambda k: rdr, rdr)
    rws = Lane(rw_s, rw_r)
    for r in range(7):
        rws.add(str(r), lambda k: rdo.at[0], lambda k, r=r: rdw.at[r], dev_w[r],
                lambda k, r=r: rdw.at[r], rdr)

    def rd_1():
        ones = jnp.ones((8, BLK), F32)
        for half in range(2):
            rdo[half] = lax.dot_general(
                ones,
                rdacc[half * TOK : (half + 1) * TOK],
                (((1,), (1,)), ((), ())),
                precision=lax.Precision.HIGHEST,
                preferred_element_type=F32,
            )
        rds.start("s", 0)

    def rd_2():
        rds.arrived("s", 0)
        rdo[0] = rdo[0] + rdr[...]
        for r in range(7):
            rws.start(str(r), 0)

    def rd_3():
        load_tsl.wait()
        for r in range(7):
            rws.arrived(str(r), 0)
        total = rdo[0]
        for r in range(7):
            total = total + rdw[r]
        rdacc[pl.ds(0, TOK)] = jnp.broadcast_to((total / D).T[:, :1], (TOK, BLK))

    rotation = hadamard()

    def decoded(core, k):
        at = wide_cols(core, k)
        turned = jnp.dot(cod[:, at], rotation, preferred_element_type=F32)
        block = core * CH + k
        norm = 1.0 / (BLK**0.5)
        top = turned[:BLK] * (grid[codes[0, block]] * norm)
        low = turned[BLK:] * (grid[codes[1, block]] * norm)
        return jnp.concatenate([top, low], axis=0).astype(BF16)

    def decode(k):
        wsib[:, cols(k)] = decoded(1 - c, k)
        swap.start("w", k)
        w[yl, z, mine, cols(k)] = decoded(c, k)

    decode(0)
    ag_own(0, "mine")

    @pl.loop(1, CH)
    def _(k):
        decode(k)

    swap.arrived("w", 0)
    ag_own(0, "other")
    for i in range(1, LA):
        ag_a(i)

    cts.start("c", 0)

    def norm_tokens():
        rdacc[...] = jnp.zeros_like(rdacc)
        load_tok.wait()

        @pl.loop(0, NB)
        def _(j):
            @pl.loop(0, TB // 32)
            def _(i):
                rows = pl.ds(pl.multiple_of(j * TB + i * 32, 32), 32)
                values = ng[rows].astype(F32)
                scale = lax.rsqrt(
                    jnp.sum(values * values, axis=-1, keepdims=True) * (1.0 / D) + 1e-5
                )
                inv[rows] = jnp.broadcast_to(scale, (32, BLK))
                normed[rows] = (values * scale * gain[...]).astype(BF16)

            nms.start("n", j)

        load_cot.wait()

    def inputs_here():
        cts.arrived("c", 0)
        @pl.loop(0, NB)
        def _(j):
            nms.arrived("n", j)

    def at_step(s, fn, first, count, each=1):
        @pl.when((s >= first) & (s < first + count // each))
        def _():
            if each == 1:
                fn(s - first)
            else:

                @pl.loop(0, each)
                def _(i):
                    fn((s - first) * each + i)

    def once(s, fn, step):
        @pl.when(s == step)
        def _():
            fn()

    def several(fn, k, count):
        @pl.loop(0, count)
        def _(i):
            fn(k + i)

    done = CH - 1 + LD

    @pl.loop(0, STEPS)
    def _(s):
        at_step(s, lambda k: ag_a(k + LA), 0, CH - LA)
        at_step(s, ag_b, 0, CH)
        at_step(s, ag_c, LC, CH)
        once(s, norm_tokens, 0)
        once(s, inputs_here, LD)
        once(s, lambda: several(rs_a, 0, RE), CH - 1)
        once(s, lambda: several(rs_a, RE, 4 - RE), CH)
        once(s, lambda: weight_part(6), done + 1)
        once(s, lambda: several(rs_a, 4, 3), done + 1)
        at_step(s, lambda k: rs_b(k + 2), done + 1, CH - 2)
        once(s, sibs_here, done + NR)
        at_step(s, ng_r, done + NR, NB, ER)
        at_step(s, rs_c, done + RC, CH)
        at_step(s, ng_u, done + NU, NB, EU)
        once(s, rd_1, done + 2)
        once(s, rd_2, done + 3)
        once(s, rd_3, done + 4)
        at_step(s, ng_v, done + NV, NB, EU)
        at_step(s, rs_d, done + RD, CH)
        once(s, lambda: several(weight_part, 0, 2), LD + 2)
        once(s, lambda: several(weight_part, 2, 2), LD + 4)
        once(s, lambda: weight_part(5), done)
        at_step(s, ag_d, LD, CH)

        @pl.when((s > LD) & (s < done) & ((s - LD) % 2 == 1))
        def _():
            forward(s - LD - 1, 2)

        at_step(s, ng_first, LD + 3, 4, 2)
        once(s, lambda: weight_part(4), CH)
        once(s, lambda: forward(CH - 1, 1), done)

        @pl.when(s == done)
        def _():
            @pl.loop(0, 2)
            def _(i):
                rs_b(i)
                several(ng_p, 2 * i, 2)

            ng_q()

    for lane in (swap, ag, rs, nms, xs, sib, cts, rds, rws):
        lane.drain()

    @pl.loop(0, CH)
    def _(k):
        act_local(k).wait()
        act_remote(k).wait_send()
        act_remote(k, True).wait_recv()
        wg_local(k).wait()
        wg_remote(k).wait_send()
        wg_remote(k, True).wait_recv()

    @pl.loop(0, NB)
    def _(j):
        ig_copy(j).wait()


def hand_over(act, wg, ig, act_out, wg_out, ig_out, act_v, wg_v, ig_v, sems):
    loads, stores = [], []
    for i, (src, mid, dst) in enumerate(
        ((act, act_v, act_out), (wg, wg_v, wg_out), (ig, ig_v, ig_out))
    ):
        rows = src.shape[0] // PARTS
        for part in range(PARTS):
            at = pl.ds(part * rows, rows)
            loads.append(pltpu.make_async_copy(src.at[at], mid.at[at], sems.at[0, i, part]))
            stores.append(pltpu.make_async_copy(mid.at[at], dst.at[at], sems.at[1, i, part]))
    for load in loads:
        load.start()
    for load, store in zip(loads, stores):
        load.wait()
        store.start()
    for store in stores:
        store.wait()


def per_device(tokens, norm_gain, coded, block_codes, grid, cotangent):
    anywhere = pl.BlockSpec(memory_space=pl.ANY)
    vmem = pl.BlockSpec(memory_space=pltpu.VMEM)
    smem = pl.BlockSpec(memory_space=pltpu.SMEM)
    sem = pltpu.SemaphoreType.DMA
    results = pl.pallas_call(
        kernel,
        out_shape=(
            jax.ShapeDtypeStruct((TOK, CW), BF16),
            jax.ShapeDtypeStruct((D // 16, CW), F32),
            jax.ShapeDtypeStruct((TOK, WS), BF16),
        ),
        in_specs=[anywhere, vmem, anywhere, smem, smem, anywhere],
        out_specs=(anywhere, anywhere, anywhere),
        scratch_shapes=[
            pltpu.VMEM((256, CW), BF16),
            pltpu.VMEM((256, HALF), BF16),
            pltpu.VMEM((2, 4, CR, HALF), BF16),
            pltpu.VMEM((2 * TOK, D), BF16),
            pltpu.VMEM((2 * TOK, HALF), BF16),
            pltpu.VMEM((2 * TOK, HALF), BF16),
            pltpu.VMEM((2, 4, CR, HALF), BF16),
            pltpu.VMEM((CR, HALF), F32),
            pltpu.VMEM((2 * TOK, D), BF16),
            pltpu.VMEM((TOK, D), BF16),
            pltpu.VMEM((2, TOK, WS), BF16),
            pltpu.VMEM((2, TOK, XS), BF16),
            pltpu.VMEM((TOK, WS), BF16),
            pltpu.VMEM((TOK, WS), BF16),
            pltpu.VMEM((TOK, WS), F32),
            pltpu.VMEM((TOK, WS), BF16),
            pltpu.VMEM((TOK, WS), BF16),
            pltpu.VMEM((TOK, BLK), F32),
            pltpu.VMEM((2 * TOK, BLK), F32),
            pltpu.VMEM((2, 8, TOK), F32),
            pltpu.VMEM((8, TOK), F32),
            pltpu.VMEM((7, 8, TOK), F32),
            pltpu.VMEM((CH, 4, R1, BLK), BF16),
            pltpu.VMEM((2, CH, 2, H2, BLK), BF16),
            pltpu.VMEM((2, CH, H1, BLK), BF16),
            pltpu.VMEM((2, CH, 2, R2, BLK), BF16),
            pltpu.VMEM((2, CH, R1, BLK), BF16),
            pltpu.VMEM((CH, R2, BLK), BF16),
            sem((4,)), sem((3, CH)), sem((3, CH)), sem((NB,)),
            sem((15,)), sem((15, CH)), sem((10,)), sem((10, CH)), sem((1,)), sem((1, 4)),
            sem((1,)), sem((1, CH)), sem((1,)), sem((1, NB)), sem((5,)), sem((5, NB)),
            sem((1,)), sem((1, 1)), sem((7,)), sem((7, 1)), sem((1,)), sem((1, 1)),
        ],
        compiler_params=pltpu.CompilerParams(
            collective_id=0, has_side_effects=True, vmem_limit_bytes=63 << 20
        ),
        cost_estimate=pl.CostEstimate(
            flops=6 * TOK * D * CW, bytes_accessed=40 << 20, transcendentals=TOK * CW
        ),
    )(tokens, norm_gain.reshape(1, D), coded, block_codes, grid, cotangent)
    return pl.pallas_call(
        hand_over,
        out_shape=tuple(jax.ShapeDtypeStruct(r.shape, r.dtype) for r in results),
        in_specs=[anywhere] * 3,
        out_specs=(anywhere,) * 3,
        scratch_shapes=[pltpu.VMEM(r.shape, r.dtype) for r in results] + [sem((2, 3, PARTS))],
        compiler_params=pltpu.CompilerParams(vmem_limit_bytes=63 << 20),
    )(*results)


def solution(mesh):
    placed = (
        P("narrow", None), P(), P("narrow", "wide"), P("narrow", "wide"), P(), P("narrow", "wide"),
    )
    return jax.shard_map(
        per_device,
        mesh=mesh,
        in_specs=placed,
        out_specs=(P("narrow", "wide"), P("narrow", "wide"), P("narrow", "wide")),
        check_vma=False,
    )
```
